32 devices in a mesh: groups: 2 (over x), solver: 8 (over z, y), trainer: 2 (over core).
Axes of the slice: x: 2, y: 2, z: 4, core: 2. Of those that a mesh axis runs over, the one named last changes fastest.
Arguments:
- initial_field: float32 [512, 8192], P(('groups', 'solver'), 'trainer'), parts along dimension 0, may hold values from -40 to 40
- coef_index: int32 [512, 8192], P(('groups', 'solver'), 'trainer'), parts along dimension 0, may hold values from 0 to 15
- kappa_table: float32 [32], P('groups'), parts along dimension 0, may hold values from 0.02 to 0.15
- drift_table: float32 [4, 16], P('groups'), parts along dimension 0, may hold values from -0.2 to 0.2
- tile_pos: int32 [4, 8, 2, 24], P('groups', 'solver', 'trainer'), parts along dimension 0, may hold values from 0 to 255
- tile_dest: int32 [4, 8, 2, 24, 1], P('groups', 'solver', 'trainer'), parts along dimension 0, may hold values from 0 to 7; in each aligned block of 24 rows (0 to 23, 24 to 47, ..., all dimensions but the last counted through in order) at most 4 rows name the same one
- conv_in: float32 [18, 64, 4], P('groups'), parts along dimension 0, may hold values from -1 to 1
- mix_weight: float32 [128, 64], P('groups'), parts along dimension 0, may hold values from -0.75 to 0.75
- conv_out: float32 [18, 1, 64], P('groups'), parts along dimension 0, may hold values from -0.25 to 0.25
Outputs:
- final_field: float32 [512, 8192], P(('groups', 'solver'), 'trainer'), parts along dimension 0
- conv_in_change: float32 [18, 64, 4], P('groups'), parts along dimension 0
- mix_change: float32 [128, 64], P('groups'), parts along dimension 0
- conv_out_change: float32 [18, 1, 64], P('groups'), parts along dimension 0
The draws below stay inside these ranges and needn't reach their ends.
There are 2 independent parts, one for each index of `groups`. The reference program is written for one: setup_inputs(seed, part) draws one part's arguments, and reference() takes and returns one part's arrays. A program takes and returns all parts, laid end to end along the dimension named above; each array names one. Nothing has to cross between parts.
Inputs may be any that keep to these rules, and one draw needn't show every extreme that they name: `tile_dest`: in each aligned block of 24 rows (one snapshot of one device) no buffer is named more than 4 times.
All inputs are finite; a program needn't handle non-finite values.
Results may differ from the reference program's by a relative error of at most 0.0003.
Values sent between devices are 32-bit elements; how exact they have to be, the bound alone decides.
No kernel may reach another device: no remote copies, remote signals or barrier semaphores. Data moves between devices by JAX's collectives and lax.ppermute only.
A program may use at most 128 MiB of HBM per device.

```python
import math
import jax
import jax.numpy as jnp
import numpy as np
from jax import lax

ROWS_DEV = 32
NY = 8192
TR = 4
TW = 128
CHANNELS = 64
NCOEF = 16
SNAPS = 2
SEND = 24
MOST = 4
NX = 256
N_SOLVER = 8
N_TRAINER = 2


def draw_initial_field(key, part):
    key = jax.random.fold_in(key, 11)
    row_key, col_key, cell_key = jax.random.split(key, 3)
    row_scale = jnp.exp(jax.random.uniform(row_key, (NX, 1), jnp.float32, 0.0, 1.0) * math.log(10.0) * 0.5)
    col_scale = jnp.exp(jax.random.uniform(col_key, (1, NY), jnp.float32, 0.0, 1.0) * math.log(10.0) * 0.5)
    cells = jax.random.truncated_normal(cell_key, -4.0, 4.0, (NX, NY), jnp.float32)
    return cells * row_scale * col_scale


def with_ends(values, stream_key, low, top_value):
    longest = values.shape.index(max(values.shape))
    spots = []
    for shift in (0, 1):
        where = [jax.random.randint(jax.random.fold_in(stream_key, axis), (), 0, length) for axis, length in enumerate(values.shape)]
        where[longest] = (where[longest] + shift) % values.shape[longest]
        spots.append(tuple(where))
    return values.at[spots[0]].set(low).at[spots[1]].set(top_value)


def deal_out(stream_key, own, number, rows, amount, top, most, lean):
    sequence = jax.random.permutation(stream_key, amount)
    heavy_load, usual = shares(amount, rows * top, most, lean, True), shares(amount, rows * top, most, lean, False)
    places = jnp.arange(amount)

    def named(sizes, rotation):
        used = int((sizes > 0).sum())
        fixed = max(1, used // 4)
        moved = fixed + (places - fixed + rotation * (used - fixed)) % max(1, amount - fixed)
        return jnp.zeros((amount,), jnp.int32).at[sequence[jnp.where(places < fixed, places, moved)]].set(jnp.asarray(sizes, jnp.int32))

    sizes = jnp.where(number % 4 == 0, named(heavy_load, number // 4), named(usual, number - number // 4 - 1))
    mixed = jax.random.permutation(jax.random.fold_in(own, 3), amount)
    giver, taker = mixed[0:amount // 2 * 2:2], mixed[1:amount // 2 * 2:2]
    slack = jnp.minimum(sizes[giver] - 1, most - sizes[taker]) // 2
    slack = jnp.where((giver == sequence[0]) | (taker == sequence[0]) | (sizes[taker] == 0), 0, jnp.maximum(slack, 0))
    moved = jax.random.randint(jax.random.fold_in(own, 4), (amount // 2,), 0, 1 << 20) % (slack + 1)
    sizes = sizes.at[giver].add(-moved).at[taker].add(moved)
    members = jnp.searchsorted(jnp.cumsum(sizes), jnp.arange(rows * top), side="right").astype(jnp.int32)
    grid = members.reshape(top, rows).T
    grid = grid[jax.random.permutation(jax.random.fold_in(own, 1), rows)]
    rotation = jax.random.randint(jax.random.fold_in(own, 2), (rows, 1), 0, top)
    return jnp.take_along_axis(grid, (jnp.arange(top)[None, :] + rotation) % top, axis=1)


def shares(amount, total, bound, skew, full):
    loads = [(1 << 20) // math.isqrt(grade ** skew) + 1 for grade in range(1, amount + 1)]
    largest = bound if full else min(bound, max(-(-total // amount), total * loads[0] // sum(loads)))
    least = 1 if total - largest >= amount - 1 else 0
    holding, spare = [largest] + [least] * (amount - 1), total - largest - least * (amount - 1)
    while spare > 0:
        movable = [i for i in range(1, amount) if holding[i] < largest] or [i for i in range(1, amount) if holding[i] < bound]
        pool, budget = sum([loads[i] for i in movable]), spare
        for i in movable:
            more = min(bound - holding[i], max(1, budget * loads[i] // pool), spare)
            holding[i] = holding[i] + more
            spare = spare - more
    return np.array(holding)


def noise(stream_key, dims, width, limit, kind=jnp.bfloat16):
    return jnp.clip(width * jax.random.normal(stream_key, dims, jnp.float32), -limit, limit).astype(kind)


def setup_inputs(seed: int = 0, part: int = 0) -> dict:
    keys = jax.random.split(jax.random.key(seed), 10)
    part_splits = jax.random.split(jax.random.fold_in(keys[9], part), 10)
    initial_field = draw_initial_field(jax.random.fold_in(jax.random.fold_in(keys[9], part), 71), part)
    coef_index = with_ends(jax.random.randint(part_splits[1], (NX, NY), 0, NCOEF), jax.random.fold_in(part_splits[1], 1), 0, NCOEF - 1).astype(jnp.int32)
    kappa_table = jnp.clip(jnp.exp(jax.random.uniform(part_splits[2], (NCOEF,), jnp.float32, math.log(0.02), math.log(0.15))), 0.02, 0.15)
    drift_table = jnp.clip(jax.random.uniform(part_splits[3], (2, NCOEF), jnp.float32, -0.2, 0.2), -0.2, 0.2)
    tile_pos = with_ends(jax.random.randint(part_splits[4], (SNAPS, N_SOLVER, N_TRAINER, SEND), 0, (ROWS_DEV // TR) * (NY // N_TRAINER // TW)), jax.random.fold_in(part_splits[4], 1), 0, ((ROWS_DEV // TR) * (NY // N_TRAINER // TW)) - 1).astype(jnp.int32)
    tile_dest_keys = jax.random.split(jax.random.fold_in(part_splits[5], 1), SNAPS * N_SOLVER * N_TRAINER * SEND // SEND)
    tile_dest_turns = jax.random.permutation(jax.random.fold_in(part_splits[5], 3), SNAPS * N_SOLVER * N_TRAINER * SEND // SEND)
    tile_dest = jax.vmap(lambda own, number: deal_out(jax.random.fold_in(part_splits[5], 2), own, number, SEND, N_SOLVER, 1, MOST, 2))(tile_dest_keys, tile_dest_turns).reshape((SNAPS, N_SOLVER, N_TRAINER, SEND, 1))
    conv_in = noise(part_splits[6], (9, CHANNELS, 4), 36 ** -0.5, 1.0, jnp.float32)
    mix_weight = noise(part_splits[7], (CHANNELS, CHANNELS), CHANNELS ** -0.5, 0.75, jnp.float32)
    conv_out = noise(part_splits[8], (9, 1, CHANNELS), (9 * CHANNELS) ** -0.5, 0.25, jnp.float32)
    return {"initial_field": initial_field, "coef_index": coef_index, "kappa_table": kappa_table, "drift_table": drift_table, "tile_pos": tile_pos, "tile_dest": tile_dest, "conv_in": conv_in, "mix_weight": mix_weight, "conv_out": conv_out}


HIGH = lax.Precision.HIGHEST
STEP_RATE = 0.05
NORM_EPS = 1e-06

def coefficients(cell_index, kappa_table, drift_table):
    diffusion = jnp.zeros(cell_index.shape, jnp.float32)
    drift_rows = jnp.zeros(cell_index.shape, jnp.float32)
    drift_cols = jnp.zeros(cell_index.shape, jnp.float32)
    for entry in range(kappa_table.shape[0]):
        chosen = cell_index == entry
        diffusion = jnp.where(chosen, kappa_table[entry], diffusion)
        drift_rows = jnp.where(chosen, drift_table[0, entry], drift_rows)
        drift_cols = jnp.where(chosen, drift_table[1, entry], drift_cols)
    return (diffusion, drift_rows, drift_cols)

def advance(padded, diffusion, drift_rows, drift_cols):
    center = padded[1:-1, 1:-1]
    above = padded[:-2, 1:-1]
    below = padded[2:, 1:-1]
    left_side = padded[1:-1, :-2]
    right_side = padded[1:-1, 2:]
    laplace = above + below + left_side + right_side - 4.0 * center
    upwind = jnp.maximum(drift_rows, 0.0) * (center - above) + jnp.minimum(drift_rows, 0.0) * (below - center)
    upwind = upwind + jnp.maximum(drift_cols, 0.0) * (center - left_side) + jnp.minimum(drift_cols, 0.0) * (right_side - center)
    return center + diffusion * laplace - upwind

def convolve(inputs, kernel):
    padded = jnp.pad(inputs, ((0, 0), (0, 0), (1, 1), (1, 1)))
    height = inputs.shape[2]
    breadth = inputs.shape[3]
    summed = jnp.zeros((kernel.shape[1], inputs.shape[1], height, breadth), jnp.float32)
    for row_shift in range(3):
        for col_shift in range(3):
            window = padded[:, :, row_shift:row_shift + height, col_shift:col_shift + breadth]
            summed = summed + jnp.einsum('oc,cbrw->obrw', kernel[3 * row_shift + col_shift], window, precision=HIGH)
    return summed

def surrogate(params, tiles):
    inputs = jnp.transpose(tiles[:, 0:4], (1, 0, 2, 3))
    first = jax.nn.gelu(convolve(inputs, params[0]))
    second = jax.nn.gelu(jnp.einsum('oc,cbrw->obrw', params[1], first, precision=HIGH))
    return tiles[:, 0] + convolve(second, params[2])[0]

def tile_loss(params, tiles, weights):
    misfit = surrogate(params, tiles) - tiles[:, 4]
    return jnp.sum(weights[:, None, None] * misfit * misfit)

def flatten(tree):
    return jnp.concatenate([leaf.reshape(-1) for leaf in tree])

def unflatten(vector, params):
    pieces = []
    offset = 0
    for weight in params:
        entries = weight.size
        pieces.append(vector[offset:offset + entries].reshape(weight.shape))
        offset = offset + entries
    return tuple(pieces)

def tile_grads(params, tiles):

    def one_tile(single):
        ones = jnp.ones((1,), jnp.float32)
        return flatten(jax.grad(tile_loss)(params, single[None], ones))
    return jax.vmap(one_tile)(tiles)

def buffer_grads(params, tiles, buffer_ids, buffers, block):
    blocks_total = tiles.shape[0] // block
    tile_blocks = tiles.reshape((blocks_total, block) + tiles.shape[1:])
    id_blocks = buffer_ids.reshape(blocks_total, block)
    flat_count = sum((weight.size for weight in params))

    def accumulate(running, portion):
        per_tile = tile_grads(params, portion[0])
        onehot_buffer = (portion[1][None, :] == jnp.arange(buffers, dtype=jnp.int32)[:, None]).astype(jnp.float32)
        added = jnp.dot(onehot_buffer, per_tile, precision=HIGH, preferred_element_type=jnp.float32)
        return (running + added, None)
    starting = jnp.zeros((buffers, flat_count), jnp.float32)
    summed, unused = lax.scan(accumulate, starting, (tile_blocks, id_blocks))
    return summed

def reference(initial_field, coef_index, kappa_table, drift_table, tile_pos, tile_dest, conv_in, mix_weight, conv_out):
    diffusion, drift_rows, drift_cols = coefficients(coef_index, kappa_table, drift_table)
    fields = [initial_field]
    current = initial_field
    for step_number in range(4):
        current = advance(jnp.pad(current, 1), diffusion, drift_rows, drift_cols)
        fields.append(current)
    per_row = NY // N_TRAINER // TW
    buffers = N_SOLVER * N_TRAINER
    params = (conv_in, mix_weight, conv_out)
    total = jnp.zeros((flatten(params).shape[0],), jnp.float32)
    for snapshot in range(SNAPS):
        stacked = jnp.stack([fields[2 * snapshot + 1], diffusion, drift_rows, drift_cols, fields[2 * snapshot + 2]])
        shaped = stacked.reshape(5, N_SOLVER, ROWS_DEV // TR, TR, N_TRAINER, per_row, TW)
        shaped = jnp.transpose(shaped, (1, 4, 2, 5, 0, 3, 6))
        shaped = shaped.reshape(N_SOLVER, N_TRAINER, ROWS_DEV // TR * per_row, 5, TR, TW)
        picks = jnp.take_along_axis(shaped, tile_pos[snapshot][:, :, :, None, None, None].astype(jnp.int32), axis=2)
        trainer_ids = jnp.arange(N_TRAINER, dtype=jnp.int32)[None, :, None]
        buffer_ids = (tile_dest[snapshot][..., 0].astype(jnp.int32) * N_TRAINER + trainer_ids).reshape(-1)
        flat_tiles = picks.reshape(N_SOLVER * N_TRAINER * SEND, 5, TR, TW)
        summed = buffer_grads(params, flat_tiles, buffer_ids, buffers, 64)
        scales = lax.rsqrt(lax.optimization_barrier(jnp.mean(summed * summed, axis=1)) + NORM_EPS)
        direction = lax.optimization_barrier(jnp.sum(summed * scales[:, None], axis=0)) / buffers
        total = total + direction
        params = tuple((weight - STEP_RATE * change for weight, change in zip(params, unflatten(direction, params))))
    changes = unflatten(total, params)
    return (fields[4], changes[0], changes[1], changes[2])
```

```python
import functools

import jax
import jax.numpy as jnp
from jax import lax
from jax.experimental import pallas as pl
from jax.experimental.pallas import tpu as pltpu
from jax.sharding import PartitionSpec as P

TR = 4
TW = 128
SNAPS = 2
STEPS = 4
EXT = 128
LIVE = 64
BATCH = 6

F32 = jnp.float32
BF16 = jnp.bfloat16
STEP_RATE = 0.05
NORM_EPS = 1e-06
GELU_A = 0.7978845608028654
GELU_B = 0.044715

VMEM = pl.BlockSpec(memory_space=pltpu.VMEM)
SMEM = pl.BlockSpec(memory_space=pltpu.SMEM)
PARAMS = pltpu.CompilerParams(vmem_limit_bytes=40 * 1024 * 1024)


def field_kernel(
    sizes, place, tile_pos, tile_dest, u0, index, ext, above, below, tables, picks, final, xin, base, slots,
    counts, fields, ids, coef,
):
    rows, lanes, sends, per_row, half = sizes
    tall = rows + 2 * STEPS
    wide = lanes + EXT
    columns = wide // 128

    ids[0:rows, 0:lanes] = index[...] + 1
    ids[0:rows, lanes:wide] = ext[1].astype(jnp.int32)
    ids[rows : rows + STEPS, :] = below[1].astype(jnp.int32)
    ids[rows + STEPS : tall, :] = above[1].astype(jnp.int32)
    fields[0, 0:rows, 0:lanes] = u0[...]
    fields[0, 0:rows, lanes:wide] = ext[0]
    fields[0, rows : rows + STEPS, :] = below[0]
    fields[0, rows + STEPS : tall, :] = above[0]

    table = [jnp.broadcast_to(tables[k : k + 1, :], (8, 128)) for k in range(4)]
    for c in range(columns):
        for r in range(tall // 8):
            here = (slice(8 * r, 8 * r + 8), slice(128 * c, 128 * c + 128))
            which = ids[here]
            for k in range(4):
                coef[(k,) + here] = jnp.take_along_axis(table[k], which, axis=1)

    lane = lax.broadcasted_iota(jnp.int32, (tall, 128), 1)
    for step in range(STEPS):
        cut = [slice(128 * c, 128 * c + 128) for c in range(columns)]
        shifted = lambda c, by: pltpu.roll(fields[step, :, cut[c % columns]], by % 128, 1)
        before, first = shifted(-1, 1), shifted(0, -1)
        ahead = first
        for c in range(columns):
            center = fields[step, :, cut[c]]
            up = pltpu.roll(center, 1, 0)
            down = pltpu.roll(center, tall - 1, 0)
            own = shifted(c, 1)
            left = jnp.where(lane == 0, before, own)
            following = shifted(c + 1, -1) if c + 1 < columns else first
            right = jnp.where(lane == 127, following, ahead)
            before, ahead = own, following
            new = (
                center
                + coef[0, :, cut[c]] * (up - center)
                + coef[1, :, cut[c]] * (down - center)
                + coef[2, :, cut[c]] * (left - center)
                + coef[3, :, cut[c]] * (right - center)
            )
            fields[step + 1, :, cut[c]] = new
            if step + 1 == STEPS and c < lanes // 128:
                final[:, cut[c]] = new[0:rows]

    mine = place[0] // half
    xin[...] = jnp.zeros_like(xin)
    base[...] = jnp.zeros_like(base)
    sub = lax.broadcasted_iota(jnp.int32, (8, 128), 0)
    channel = picks[...]
    for snapshot in range(SNAPS):
        before, after = 2 * snapshot + 1, 2 * snapshot + 2

        def pick(k, filled):
            far, near = filled
            dest = tile_dest[snapshot, k]
            away = dest // half != mine
            slot = jnp.where(away, far, sends + near)
            slots[snapshot, slot] = lax.rem(dest, half)
            where = tile_pos[snapshot, k]
            top = lax.div(where, per_row) * TR
            start = pl.multiple_of(lax.rem(where, per_row) * TW, TW)
            spot = (pl.ds(pl.multiple_of(top // 8 * 8, 8), 8), pl.ds(start, TW))
            lower = lax.rem(top, 8) == TR
            tile = lambda x: jnp.where(lower, pltpu.roll(x, TR, 0), x)
            value = tile(fields[(before,) + spot])
            which = tile(ids[spot])
            base[snapshot, slot] = (value - tile(fields[(after,) + spot]))[0:TR]
            for r in range(TR):
                row = lambda x: jnp.broadcast_to(x[r : r + 1], (8, 128))
                found = jnp.take_along_axis(channel, row(which), axis=1)
                xin[snapshot, slot, r] = jnp.where(sub % 4 == 0, row(value), found)
            return (jnp.where(away, far + 1, far), jnp.where(away, near, near + 1))

        far, near = lax.fori_loop(0, sends, pick, (jnp.int32(0), jnp.int32(0)))
        counts[snapshot, 0] = far
        counts[snapshot, 1] = near


def split(x):
    high = x.astype(BF16)
    return high, (x - high.astype(F32)).astype(BF16)


def weights3(w):
    high = w.astype(BF16).astype(F32)
    return jnp.concatenate([high, high, w - high], axis=1).astype(BF16)


def values3(high, low):
    return jnp.concatenate([high, low, high], axis=0)


def times(a, b):
    return lax.dot_general(a, b, (((1,), (0,)), ((), ())), preferred_element_type=F32)


def over_cells(a, b):
    return lax.dot_general(a, b, (((1,), (1,)), ((), ())), preferred_element_type=F32)


def gelu_and_slope(z):
    square = z * z
    t = jnp.tanh(z * (GELU_A + (GELU_A * GELU_B) * square))
    gate = 0.5 + 0.5 * t
    value = z * gate
    return value, gate + (value - value * gate) * (2 * GELU_A + (6 * GELU_A * GELU_B) * square)


def lane_shift(x, by):
    lane = lax.broadcasted_iota(jnp.int32, x.shape, 1)
    return jnp.where(lane == (0 if by == 1 else TW - 1), 0.0, pltpu.roll(x, by % TW, 1))


def batch_gradients(cells, gaps, weights):
    w1, mix, w3, w3_t, mix_t = weights
    number = len(cells)
    zero8 = jnp.zeros((8, TW), F32)
    sub8 = lax.broadcasted_iota(jnp.int32, (8, TW), 0)
    columns = []
    for tile in cells:
        sides = [jnp.where(sub8 < 4, lane_shift(x, 1), lane_shift(x, -1)) for x in tile]
        sides = [zero8] + sides + [zero8]
        center = [zero8] + list(tile) + [zero8]
        for r in range(TR):
            stacked = []
            for dr in range(3):
                stacked += [sides[r + dr], center[r + dr]]
            columns.append(jnp.concatenate(stacked, axis=0))
    x_hi, x_lo = split(jnp.concatenate(columns, axis=1))
    h1, slope1 = gelu_and_slope(times(w1, values3(x_hi, x_lo)))
    h1_hi, h1_lo = split(h1)
    h2, slope2 = gelu_and_slope(times(mix, values3(h1_hi, h1_lo)))
    h2_hi, h2_lo = split(h2)
    taps = times(w3, values3(h2_hi, h2_lo))

    sub = lax.broadcasted_iota(jnp.int32, (16, TW), 0)
    tap_col, tap_row = lax.rem(sub, 3), lax.div(sub, 3)
    zero16 = jnp.zeros((16, TW), F32)

    def by_col(x, by):
        return jnp.where(
            tap_col == 0, lane_shift(x, by), jnp.where(tap_col == 2, lane_shift(x, -by), x)
        )

    def by_row(first, middle, last):
        return jnp.where(
            tap_row == 0, first, jnp.where(tap_row == 1, middle, jnp.where(tap_row == 2, last, 0.0))
        )

    spread = []
    for t in range(number):
        moved = [zero16]
        for r in range(TR):
            at = (t * TR + r) * TW
            moved.append(by_col(taps[:, at : at + TW], 1))
        moved.append(zero16)
        errors = [zero16]
        for r in range(TR):
            summed = jnp.sum(by_row(moved[r], moved[r + 1], moved[r + 2]), axis=0, keepdims=True)
            errors.append(by_col(jnp.broadcast_to(2.0 * (summed + gaps[t][r]), (16, TW)), -1))
        errors.append(zero16)
        spread += [by_row(errors[r + 2], errors[r + 1], errors[r]) for r in range(TR)]
    e_hi, e_lo = split(jnp.concatenate(spread, axis=1))
    d2_hi, d2_lo = split(times(w3_t, values3(e_hi, e_lo)) * slope2)
    d1_hi, d1_lo = split(times(mix_t, values3(d2_hi, d2_lo)) * slope1)

    result = []
    for t in range(number):
        own = slice(t * TR * TW, (t + 1) * TR * TW)
        both = lambda high, low: jnp.concatenate([high[:, own], low[:, own]], axis=0)
        result.append(
            jnp.concatenate(
                [
                    over_cells(both(d2_hi, d2_lo), both(h1_hi, h1_lo)),
                    over_cells(both(x_hi, x_lo), both(d1_hi, d1_lo)),
                    over_cells(both(e_hi, e_lo), both(h2_hi, h2_lo)),
                ],
                axis=0,
            )
        )
    return result


def gradient_kernel(snapshot, part, sends, slots, counts, xin, base, params, out, total):
    buffers = out.shape[0]
    total[...] = jnp.zeros_like(total)
    packed = params[...]
    mix = packed[:, 0:64]
    w1 = packed[0:48, 64:128]
    w3 = packed[48:64, 64:128]
    weights = (weights3(w1.T), weights3(mix), weights3(w3), weights3(w3.T), weights3(mix.T))

    def body(i, carry):
        at = [part * sends + i * BATCH + k for k in range(BATCH)]
        cells = [[xin[j, r] for r in range(TR)] for j in at]
        gaps = [[base[j, r : r + 1, :] for r in range(TR)] for j in at]
        number = counts[snapshot, part]
        for k, grad in enumerate(batch_gradients(cells, gaps, weights)):
            buffer = jnp.where(i * BATCH + k < number, slots[snapshot, at[k]], 0)
            total[buffer] += grad
        return carry

    lax.fori_loop(0, lax.div(counts[snapshot, part] + (BATCH - 1), BATCH), body, 0)

    row = lax.broadcasted_iota(jnp.int32, (48, 64), 0)

    def fold(b, carry):
        def parts(first, height):
            x = total[b, first : first + 2 * height, :]
            x = x[:height] + x[height:]
            return x[:, 0:64] + x[:, 64:128]

        d_w1 = jnp.where(lax.rem(row, 16) < 12, parts(128, 48), 0.0)
        out[b] = jnp.concatenate(
            [parts(0, 64), jnp.concatenate([d_w1, parts(224, 16)], axis=0)], axis=1
        )
        return carry

    lax.fori_loop(0, buffers, fold, 0)


def combine_kernel(entries, own, other, out):
    result = jnp.zeros(out.shape, F32)
    for b in range(own.shape[0]):
        full = own[b] + other[b]
        square = jnp.sum(full * full, keepdims=True)
        result = result + full * lax.rsqrt(square / entries + NORM_EPS)
    out[...] = result


def pack_weights(conv_in, mix_weight, conv_out):
    taps = conv_in.reshape(3, 3, conv_in.shape[1], 4)
    sides = jnp.concatenate([taps[:, 0], taps[:, 2], taps[:, 1], jnp.zeros_like(taps[:, 1])], axis=2)
    first = jnp.transpose(sides, (0, 2, 1)).reshape(48, conv_in.shape[1])
    last = jnp.pad(conv_out[:, 0, :], ((0, 7), (0, 0)))
    return jnp.concatenate([mix_weight, jnp.concatenate([first, last], axis=0)], axis=1)


def unpack_weights(packed):
    first = packed[0:48, 64:128].reshape(3, 4, 4, 64)
    taps = jnp.stack([first[:, 0], first[:, 2], first[:, 1]], axis=1)
    conv_in = jnp.transpose(taps.reshape(9, 4, 64), (0, 2, 1))
    return conv_in, packed[:, 0:64], packed[48:57, 64:128][:, None, :]


def local(
    initial_field,
    coef_index,
    kappa_table,
    drift_table,
    tile_pos,
    tile_dest,
    conv_in,
    mix_weight,
    conv_out,
):
    rows, lanes = initial_field.shape
    solvers = lax.axis_size("solver")
    trainers = lax.axis_size("trainer")
    half = solvers // 2
    j = lax.axis_index("solver")
    t = lax.axis_index("trainer")
    sends = tile_pos.shape[-1]
    entries = conv_in.size + mix_weight.size + conv_out.size

    def swap(x, axis, bit):
        count = lax.axis_size(axis)
        return lax.ppermute(x, axis, [(i, i ^ bit) for i in range(count)])

    both = jnp.stack([initial_field, (coef_index + 1).astype(F32)])
    edge = jnp.where(t == 0, both[:, :, lanes - EXT :], both[:, :, :EXT])
    ext = swap(edge, "trainer", 1)
    lane = lax.broadcasted_iota(jnp.int32, ext.shape, 2)
    ext = jnp.where((lane < LIVE) == (t == 0), ext, 0.0)
    down = jnp.concatenate([both[:, rows - STEPS :], ext[:, rows - STEPS :]], axis=2)
    up = jnp.concatenate([both[:, :STEPS], ext[:, :STEPS]], axis=2)
    above = lax.ppermute(down, "solver", [(i, i + 1) for i in range(solvers - 1)])
    below = lax.ppermute(up, "solver", [(i + 1, i) for i in range(solvers - 1)])

    vr, vc = drift_table[0], drift_table[1]
    coef = jnp.stack(
        [
            kappa_table + jnp.maximum(vr, 0.0),
            kappa_table - jnp.minimum(vr, 0.0),
            kappa_table + jnp.maximum(vc, 0.0),
            kappa_table - jnp.minimum(vc, 0.0),
        ]
    )
    none = jnp.zeros_like(kappa_table)
    channel = jnp.stack([none, kappa_table, vr, vc, none, kappa_table, vr, vc])
    fill = 127 - kappa_table.shape[0]
    coef = jnp.pad(coef, ((0, 4), (1, fill)))
    channel = jnp.pad(channel, ((0, 0), (1, fill)))

    sizes = (rows, lanes, sends, lanes // TW, half)
    tall, wide = rows + 2 * STEPS, lanes + EXT
    spare = -(-sends // BATCH) * BATCH
    final, xin, base, slots, counts = pl.pallas_call(
        functools.partial(field_kernel, sizes),
        out_shape=(
            jax.ShapeDtypeStruct((rows, lanes), F32),
            jax.ShapeDtypeStruct((SNAPS, sends + spare, TR, 8, TW), F32),
            jax.ShapeDtypeStruct((SNAPS, sends + spare, TR, TW), F32),
            jax.ShapeDtypeStruct((SNAPS, sends + spare), jnp.int32),
            jax.ShapeDtypeStruct((SNAPS, 2), jnp.int32),
        ),
        in_specs=[SMEM] * 3 + [VMEM] * 7,
        out_specs=(VMEM, VMEM, VMEM, SMEM, SMEM),
        scratch_shapes=[
            pltpu.VMEM((STEPS + 1, tall, wide), F32),
            pltpu.VMEM((tall, wide), jnp.int32),
            pltpu.VMEM((4, tall, wide), F32),
        ],
        compiler_params=PARAMS,
    )(
        j.reshape(1),
        tile_pos.reshape(SNAPS, sends),
        tile_dest.reshape(SNAPS, sends),
        initial_field,
        coef_index,
        ext,
        above,
        below,
        coef,
        channel,
    )

    params = pack_weights(conv_in, mix_weight, conv_out)
    change = jnp.zeros_like(params)
    work = 3 * 2 * 20000 * TR * TW * sends // 2

    def gradients(snapshot, part, params):
        return pl.pallas_call(
            functools.partial(gradient_kernel, snapshot, part, sends),
            out_shape=jax.ShapeDtypeStruct((half,) + params.shape, F32),
            in_specs=[SMEM] * 2 + [VMEM] * 3,
            out_specs=VMEM,
            scratch_shapes=[pltpu.VMEM((half, 256, 128), F32)],
            compiler_params=PARAMS,
            cost_estimate=pl.CostEstimate(
                flops=work * 16, bytes_accessed=1 << 21, transcendentals=1 << 20
            ),
        )(slots, counts, xin[snapshot], base[snapshot], params)

    for snapshot in range(SNAPS):
        far = gradients(snapshot, 0, params)
        arrived = swap(far, "solver", half)
        near = gradients(snapshot, 1, params) + arrived
        bit = 1
        while 2 * bit < half:
            near = near + swap(near, "solver", bit)
            bit = 2 * bit
        direction = pl.pallas_call(
            functools.partial(combine_kernel, entries),
            out_shape=jax.ShapeDtypeStruct(params.shape, F32),
            in_specs=[VMEM] * 2,
            out_specs=VMEM,
            compiler_params=PARAMS,
        )(near, swap(near, "solver", bit))
        direction = direction + swap(direction, "solver", half)
        direction = direction + swap(direction, "trainer", 1)
        direction = direction / (solvers * trainers)
        change = change + direction
        params = params - STEP_RATE * direction
    first, mix, last = unpack_weights(change)
    return (final, first, mix, last)


def solution(mesh):
    return jax.shard_map(
        local,
        mesh=mesh,
        in_specs=(
            P(("groups", "solver"), "trainer"),
            P(("groups", "solver"), "trainer"),
            P("groups"),
            P("groups", None),
            P("groups", "solver", "trainer", None),
            P("groups", "solver", "trainer", None, None),
            P("groups", None, None),
            P("groups", None),
            P("groups", None, None),
        ),
        out_specs=(
            P(("groups", "solver"), "trainer"),
            P("groups", None, None),
            P("groups", None),
            P("groups", None, None),
        ),
        check_vma=False,
    )
```

```python
import functools

import jax
import jax.numpy as jnp
from jax import lax
from jax.experimental import pallas as pl
from jax.experimental.pallas import tpu as pltpu
from jax.sharding import PartitionSpec as P

TR = 4
TW = 128
SNAPS = 2
STEPS = 4
EXT = 128
LIVE = 64
BATCH = 4
FIRST = 3

F32 = jnp.float32
BF16 = jnp.bfloat16
STEP_RATE = 0.05
NORM_EPS = 1e-06
GELU_A = 0.7978845608028654
GELU_B = 0.044715

VMEM = pl.BlockSpec(memory_space=pltpu.VMEM)
SMEM = pl.BlockSpec(memory_space=pltpu.SMEM)
PARAMS = pltpu.CompilerParams(vmem_limit_bytes=24 * 1024 * 1024)


def look_up(tables, which, out):
    rows = [jnp.broadcast_to(tables[k : k + 1, :], (8, 128)) for k in range(4)]
    for c in range(which.shape[1] // 128):
        for r in range(which.shape[0] // 8):
            here = (slice(8 * r, 8 * r + 8), slice(128 * c, 128 * c + 128))
            for k in range(4):
                out[(k,) + here] = jnp.take_along_axis(rows[k], which[here], axis=1)


def advance(read, coef, write, tall, columns):
    lane = lax.broadcasted_iota(jnp.int32, (tall, 128), 1)
    cut = [slice(128 * c, 128 * c + 128) for c in range(columns)]
    before = pltpu.roll(read(cut[-1]), 1, 1)
    first = pltpu.roll(read(cut[0]), 127, 1)
    ahead = first
    for c in range(columns):
        center = read(cut[c])
        own = pltpu.roll(center, 1, 1)
        left = jnp.where(lane == 0, before, own)
        following = pltpu.roll(read(cut[c + 1]), 127, 1) if c + 1 < columns else first
        right = jnp.where(lane == 127, following, ahead)
        before, ahead = own, following
        up = pltpu.roll(center, 1, 0)
        down = pltpu.roll(center, tall - 1, 0)
        write(
            cut[c],
            center
            + coef(0, cut[c]) * (up - center)
            + coef(1, cut[c]) * (down - center)
            + coef(2, cut[c]) * (left - center)
            + coef(3, cut[c]) * (right - center),
        )


def inner_kernel(both, ext, tables, fields, coef, ids, start):
    rows, lanes = both.shape[1:]
    wide = lanes + EXT
    ids[:, 0:lanes] = both[1].astype(jnp.int32)
    ids[:, lanes:wide] = ext[1].astype(jnp.int32)
    start[:, 0:lanes] = both[0]
    start[:, lanes:wide] = ext[0]
    look_up(tables, ids, coef)
    for step in range(STEPS):
        source = start if step == 0 else fields.at[step - 1]
        target = fields.at[step]

        def write(cut, new):
            target[:, cut] = new

        advance(lambda cut: source[:, cut], lambda k, cut: coef[k, :, cut], write, rows, wide // 128)


def pick_tiles(snapshot, sizes, place, tile_pos, tile_dest, both, main, strip, picks, xin, base, slots, counts):
    sends, per_row, half, blocks = sizes
    mine = lax.div(place[0], half)
    sub = lax.broadcasted_iota(jnp.int32, (8, 128), 0)
    channel = picks[...]
    aways = [(lax.div(tile_dest[snapshot, k], half) != mine).astype(jnp.int32) for k in range(sends)]
    counts[0] = sum(aways)
    far, near = jnp.int32(0), sum(aways)
    for k in range(sends):
        away = aways[k]
        slot = jnp.where(away == 1, far, near)
        far, near = far + away, near + 1 - away
        slots[slot] = lax.rem(tile_dest[snapshot, k], half) + half * (1 - away)
        where = tile_pos[snapshot, k]
        block = lax.div(where, per_row)
        lanes = pl.ds(pl.multiple_of(lax.rem(where, per_row) * TW, TW), TW)
        group = pl.ds(pl.multiple_of(lax.div(block, 2) * 8, 8), 8)
        edge = (block == 0) | (block == blocks - 1)
        beside = pl.ds(pl.multiple_of(jnp.where(block == 0, 16, 0), 8), 8)
        lower = lax.rem(block, 2) == 1

        def tile(x):
            return jnp.where(lower, pltpu.roll(x, TR, 0), x)

        def value(at):
            return tile(jnp.where(edge, strip[at][beside, lanes], main[at][group, lanes]))

        old = value(0)
        which = tile(both[1, group, lanes]).astype(jnp.int32)
        base[slot] = (old - value(1))[0:TR]
        for r in range(TR):
            found = jnp.take_along_axis(channel, jnp.broadcast_to(which[r : r + 1], (8, 128)), axis=1)
            xin[slot, r] = jnp.where(sub % 4 == 0, jnp.broadcast_to(old[r : r + 1], (8, 128)), found)


def strip_coef(coef, outer, rows):
    return lambda k, cut: jnp.concatenate(
        [coef[k, rows - 8 : rows, cut], outer[k, :, cut], coef[k, 0:8, cut]], axis=0
    )


def first_strip_kernel(
    sizes, place, tile_pos, tile_dest, both, ext, first, second, tables, picks, coef, fields,
    xin, base, slots, counts, strip, outer, ids, work,
):
    rows, lanes = both.shape[1:]
    wide = lanes + EXT
    odd = lax.rem(place[0], 2) == 1
    above = [jnp.where(odd, first[k], second[k]) for k in range(2)]
    below = [jnp.where(odd, second[k], first[k]) for k in range(2)]
    ids[...] = jnp.concatenate([below[1], above[1]], axis=0).astype(jnp.int32)
    look_up(tables, ids, outer)
    work[0, 0:8, 0:lanes] = both[0, rows - 8 : rows]
    work[0, 0:8, lanes:wide] = ext[0, rows - 8 : rows]
    work[0, 8:16] = jnp.concatenate([below[0], above[0]], axis=0)
    work[0, 16:24, 0:lanes] = both[0, 0:8]
    work[0, 16:24, lanes:wide] = ext[0, 0:8]
    for step in range(2):
        source = work.at[step]
        target = work.at[1] if step == 0 else strip

        def write(cut, new):
            target[:, cut] = new

        advance(lambda cut: source[:, cut], strip_coef(coef, outer, rows), write, 24, wide // 128)
    pick_tiles(
        0, sizes, place, tile_pos, tile_dest, both, (fields.at[0], fields.at[1]), (work.at[1], strip),
        picks, xin, base, slots, counts,
    )


def second_strip_kernel(
    sizes, place, tile_pos, tile_dest, both, picks, coef, fields, strip, outer,
    final, xin, base, slots, counts, work,
):
    rows, lanes = both.shape[1:]
    wide = lanes + EXT
    for step in range(2):
        source = strip if step == 0 else work.at[0]
        target = work.at[step]

        def write(cut, new):
            target[:, cut] = new

        advance(lambda cut: source[:, cut], strip_coef(coef, outer, rows), write, 24, wide // 128)
    sub = lax.broadcasted_iota(jnp.int32, (8, lanes), 0)
    final[0:8] = jnp.where(sub < STEPS, work[1, 16:24, 0:lanes], fields[3, 0:8, 0:lanes])
    final[8 : rows - 8] = fields[3, 8 : rows - 8, 0:lanes]
    final[rows - 8 : rows] = jnp.where(sub >= 8 - STEPS, work[1, 0:8, 0:lanes], fields[3, rows - 8 : rows, 0:lanes])
    pick_tiles(
        1, sizes, place, tile_pos, tile_dest, both, (fields.at[2], fields.at[3]), (work.at[0], work.at[1]),
        picks, xin, base, slots, counts,
    )


def split(x):
    high = x.astype(BF16)
    return high, (x - high.astype(F32)).astype(BF16)


def weights3(w):
    high = w.astype(BF16).astype(F32)
    return jnp.concatenate([high, high, w - high], axis=1).astype(BF16)


def values3(high, low):
    return jnp.concatenate([high, low, high], axis=0)


def times(a, b):
    return lax.dot_general(a, b, (((1,), (0,)), ((), ())), preferred_element_type=F32)


def over_cells(a, b):
    return lax.dot_general(a, b, (((1,), (1,)), ((), ())), preferred_element_type=F32)


def gelu_and_slope(z):
    square = z * z
    t = jnp.tanh(z * (GELU_A + (GELU_A * GELU_B) * square))
    gate = 0.5 + 0.5 * t
    value = z * gate
    return value, gate + (value - value * gate) * (2 * GELU_A + (6 * GELU_A * GELU_B) * square)


def lane_shift(x, by):
    lane = lax.broadcasted_iota(jnp.int32, x.shape, 1)
    return jnp.where(lane == (0 if by == 1 else TW - 1), 0.0, pltpu.roll(x, by % TW, 1))


def batch_gradients(cells, gaps, weights):
    w1, mix, w3, w3_t, mix_t = weights
    number = len(cells)
    zero8 = jnp.zeros((8, TW), F32)
    sub8 = lax.broadcasted_iota(jnp.int32, (8, TW), 0)
    columns = []
    for tile in cells:
        sides = [jnp.where(sub8 < 4, lane_shift(x, 1), lane_shift(x, -1)) for x in tile]
        sides = [zero8] + sides + [zero8]
        center = [zero8] + list(tile) + [zero8]
        for r in range(TR):
            stacked = []
            for dr in range(3):
                stacked += [sides[r + dr], center[r + dr]]
            columns.append(jnp.concatenate(stacked, axis=0))
    x_hi, x_lo = split(jnp.concatenate(columns, axis=1))
    h1, slope1 = gelu_and_slope(times(w1, values3(x_hi, x_lo)))
    h1_hi, h1_lo = split(h1)
    h2, slope2 = gelu_and_slope(times(mix, values3(h1_hi, h1_lo)))
    h2_hi, h2_lo = split(h2)
    taps = times(w3, values3(h2_hi, h2_lo))

    sub = lax.broadcasted_iota(jnp.int32, (16, TW), 0)
    tap_col, tap_row = lax.rem(sub, 3), lax.div(sub, 3)
    zero16 = jnp.zeros((16, TW), F32)

    def by_col(x, by):
        return jnp.where(
            tap_col == 0, lane_shift(x, by), jnp.where(tap_col == 2, lane_shift(x, -by), x)
        )

    def by_row(first, middle, last):
        return jnp.where(
            tap_row == 0, first, jnp.where(tap_row == 1, middle, jnp.where(tap_row == 2, last, 0.0))
        )

    spread = []
    for t in range(number):
        moved = [zero16]
        for r in range(TR):
            at = (t * TR + r) * TW
            moved.append(by_col(taps[:, at : at + TW], 1))
        moved.append(zero16)
        errors = [zero16]
        for r in range(TR):
            summed = jnp.sum(by_row(moved[r], moved[r + 1], moved[r + 2]), axis=0, keepdims=True)
            errors.append(by_col(jnp.broadcast_to(2.0 * (summed + gaps[t][r]), (16, TW)), -1))
        errors.append(zero16)
        spread += [by_row(errors[r + 2], errors[r + 1], errors[r]) for r in range(TR)]
    e_hi, e_lo = split(jnp.concatenate(spread, axis=1))
    d2_hi, d2_lo = split(times(w3_t, values3(e_hi, e_lo)) * slope2)
    d1_hi, d1_lo = split(times(mix_t, values3(d2_hi, d2_lo)) * slope1)

    result = []
    for t in range(number):
        own = slice(t * TR * TW, (t + 1) * TR * TW)
        both = lambda high, low: jnp.concatenate([high[:, own], low[:, own]], axis=0)
        result.append(
            jnp.concatenate(
                [
                    over_cells(both(d2_hi, d2_lo), both(h1_hi, h1_lo)),
                    over_cells(both(x_hi, x_lo), both(d1_hi, d1_lo)),
                    over_cells(both(e_hi, e_lo), both(h2_hi, h2_lo)),
                ],
                axis=0,
            )
        )
    return result


def add_batches(first, last, sends, slots, xin, base, params, total):
    mix = jnp.concatenate([params[0:32, 0:64], params[0:32, 64:128]], axis=0)
    side, rest = params[32:56, 0:64], params[32:56, 64:128]
    none = jnp.zeros((8, 64), F32)
    taps = [[side[8 * r : 8 * r + 8], rest[4 * r : 4 * r + 4], none[0:4]] for r in range(3)]
    w1 = jnp.concatenate(sum(taps, []), axis=0)
    w3 = jnp.concatenate([rest[12:21], none[0:7]], axis=0)
    weights = (weights3(w1.T), weights3(mix), weights3(w3), weights3(w3.T), weights3(mix.T))

    def body(i, carry):
        at = [i * BATCH + k for k in range(BATCH)]
        cells = [[xin[j, r] for r in range(TR)] for j in at]
        gaps = [[base[j, r : r + 1, :] for r in range(TR)] for j in at]
        into = [slots[j] for j in at]
        if sends % BATCH:
            cells = [[jnp.where(j < sends, x, 0.0) for x in tile] for j, tile in zip(at, cells)]
            gaps = [[jnp.where(j < sends, x, 0.0) for x in tile] for j, tile in zip(at, gaps)]
            into = [jnp.where(j < sends, slot, 0) for j, slot in zip(at, into)]
        for buffer, grad in zip(into, batch_gradients(cells, gaps, weights)):
            total[buffer] += grad
        return carry

    lax.fori_loop(first, last, body, 0)


def fold(sums):
    def parts(first, height):
        x = sums[first : first + height, :] + sums[first + height : first + 2 * height, :]
        return x[:, 0:64] + x[:, 64:128]

    d_mix, d_w1, d_w3 = parts(0, 64), parts(128, 48), parts(224, 16)
    side = [d_w1[16 * r : 16 * r + 8] for r in range(3)]
    center = [d_w1[16 * r + 8 : 16 * r + 12] for r in range(3)]
    rest = jnp.concatenate(center + [d_w3[0:9], jnp.zeros((3, 64), F32)], axis=0)
    return jnp.concatenate(
        [
            jnp.concatenate([d_mix[0:32], d_mix[32:64]], axis=1),
            jnp.concatenate([jnp.concatenate(side, axis=0), rest], axis=1),
        ],
        axis=0,
    )


def batches_in_first(far, sends):
    return jnp.maximum(lax.div(far + (BATCH - 1), BATCH), FIRST * -(-sends // BATCH) // 4)


def first_gradient_kernel(sends, slots, counts, xin, base, params, far, total):
    half = far.shape[0]
    total[...] = jnp.zeros_like(total)
    add_batches(0, batches_in_first(counts[0], sends), sends, slots, xin, base, params, total)
    for b in range(half):
        far[b] = fold(total.at[b])


def second_gradient_kernel(sends, slots, counts, xin, base, params, begun, near, total):
    half = near.shape[0]
    total[half : 2 * half] = begun[half : 2 * half]
    last = -(-sends // BATCH)
    add_batches(batches_in_first(counts[0], sends), last, sends, slots, xin, base, params, total)
    for b in range(half):
        near[b] = fold(total.at[half + b])


def combine_kernel(entries, own, other, out):
    result = jnp.zeros(out.shape, F32)
    for b in range(own.shape[0]):
        full = own[b] + other[b]
        square = jnp.sum(full * full, keepdims=True)
        result = result + full * lax.rsqrt(square / entries + NORM_EPS)
    out[...] = result


def pack_weights(conv_in, mix_weight, conv_out):
    taps = jnp.transpose(conv_in, (0, 2, 1)).reshape(3, 3, 4, conv_in.shape[1])
    side = jnp.concatenate([taps[:, 0], taps[:, 2]], axis=1).reshape(24, conv_in.shape[1])
    rest = jnp.concatenate(
        [taps[:, 1].reshape(12, conv_in.shape[1]), jnp.pad(conv_out[:, 0, :], ((0, 3), (0, 0)))], axis=0
    )
    mix = jnp.concatenate([mix_weight[0:32], mix_weight[32:64]], axis=1)
    return jnp.concatenate([mix, jnp.concatenate([side, rest], axis=1)], axis=0)


def unpack_weights(packed):
    side = packed[32:56, 0:64].reshape(3, 2, 4, 64)
    center = packed[32:44, 64:128].reshape(3, 4, 64)
    taps = jnp.stack([side[:, 0], center, side[:, 1]], axis=1)
    conv_in = jnp.transpose(taps.reshape(9, 4, 64), (0, 2, 1))
    mix = jnp.concatenate([packed[0:32, 0:64], packed[0:32, 64:128]], axis=0)
    return conv_in, mix, packed[44:53, 64:128][:, None, :]


def local(
    initial_field,
    coef_index,
    kappa_table,
    drift_table,
    tile_pos,
    tile_dest,
    conv_in,
    mix_weight,
    conv_out,
):
    rows, lanes = initial_field.shape
    solvers = lax.axis_size("solver")
    trainers = lax.axis_size("trainer")
    half = solvers // 2
    j = lax.axis_index("solver")
    t = lax.axis_index("trainer")
    sends = tile_pos.shape[-1]
    entries = conv_in.size + mix_weight.size + conv_out.size

    def swap(x, axis, bit):
        count = lax.axis_size(axis)
        return lax.ppermute(x, axis, [(i, i ^ bit) for i in range(count)])

    both = lax.optimization_barrier(jnp.stack([initial_field, (coef_index + 1).astype(F32)]))
    ext = swap(jnp.where(t == 0, both[:, :, lanes - EXT :], both[:, :, :EXT]), "trainer", 1)
    lane = lax.broadcasted_iota(jnp.int32, ext.shape, 2)
    ext = jnp.where((lane < LIVE) == (t == 0), ext, 0.0)

    def rows_from(start):
        part = lambda x: lax.dynamic_slice_in_dim(x, start, STEPS, 1)
        return jnp.concatenate([part(both), part(ext)], axis=2)

    odd = j % 2 == 1
    last = rows - STEPS
    inner = [(i, i ^ 1) for i in range(solvers)]
    outer_pairs = [(i, i + 1) for i in range(1, solvers - 1, 2)] + [(i + 1, i) for i in range(1, solvers - 1, 2)]
    first = lax.ppermute(rows_from(jnp.where(odd, 0, last)), "solver", inner)
    second = lax.ppermute(rows_from(jnp.where(odd, last, 0)), "solver", outer_pairs)

    vr, vc = drift_table[0], drift_table[1]
    tables = jnp.stack(
        [
            kappa_table + jnp.maximum(vr, 0.0),
            kappa_table - jnp.minimum(vr, 0.0),
            kappa_table + jnp.maximum(vc, 0.0),
            kappa_table - jnp.minimum(vc, 0.0),
        ]
    )
    none = jnp.zeros_like(kappa_table)
    channel = jnp.stack([none, kappa_table, vr, vc, none, kappa_table, vr, vc])
    fill = 127 - kappa_table.shape[0]
    tables = jnp.pad(tables, ((0, 4), (1, fill)))
    channel = jnp.pad(channel, ((0, 0), (1, fill)))

    sizes = (sends, lanes // TW, half, rows // TR)
    wide = lanes + EXT
    spare = -sends % BATCH
    place = j.reshape(1)
    tile_pos = tile_pos.reshape(SNAPS, sends)
    tile_dest = tile_dest.reshape(SNAPS, sends)
    tile_shapes = (
        jax.ShapeDtypeStruct((sends + spare, TR, 8, TW), F32),
        jax.ShapeDtypeStruct((sends + spare, TR, TW), F32),
        jax.ShapeDtypeStruct((sends + spare,), jnp.int32),
        jax.ShapeDtypeStruct((1,), jnp.int32),
    )
    tile_specs = (VMEM, VMEM, SMEM, SMEM)
    fields, coef = pl.pallas_call(
        inner_kernel,
        out_shape=(
            jax.ShapeDtypeStruct((STEPS, rows, wide), F32),
            jax.ShapeDtypeStruct((4, rows, wide), F32),
        ),
        in_specs=[VMEM] * 3,
        out_specs=(VMEM, VMEM),
        scratch_shapes=[pltpu.VMEM((rows, wide), jnp.int32), pltpu.VMEM((rows, wide), F32)],
        compiler_params=PARAMS,
        cost_estimate=pl.CostEstimate(flops=1 << 31, bytes_accessed=1 << 23, transcendentals=0),
    )(both, ext, tables)
    *tiles_0, strip, outer = pl.pallas_call(
        functools.partial(first_strip_kernel, sizes),
        out_shape=tile_shapes
        + (jax.ShapeDtypeStruct((24, wide), F32), jax.ShapeDtypeStruct((4, 8, wide), F32)),
        in_specs=[SMEM] * 3 + [VMEM] * 8,
        out_specs=tile_specs + (VMEM, VMEM),
        scratch_shapes=[pltpu.VMEM((8, wide), jnp.int32), pltpu.VMEM((2, 24, wide), F32)],
        compiler_params=PARAMS,
    )(place, tile_pos, tile_dest, both, ext, first, second, tables, channel, coef, fields)

    def second_part(fields, strip):
        return pl.pallas_call(
            functools.partial(second_strip_kernel, sizes),
            out_shape=(jax.ShapeDtypeStruct((rows, lanes), F32),) + tile_shapes,
            in_specs=[SMEM] * 3 + [VMEM] * 6,
            out_specs=(VMEM,) + tile_specs,
            scratch_shapes=[pltpu.VMEM((2, 24, wide), F32)],
            compiler_params=PARAMS,
            cost_estimate=pl.CostEstimate(flops=1 << 31, bytes_accessed=1 << 23, transcendentals=0),
        )(place, tile_pos, tile_dest, both, channel, coef, fields, strip, outer)

    params = pack_weights(conv_in, mix_weight, conv_out)
    change = jnp.zeros_like(params)
    work = 3 * 2 * 20000 * TR * TW * sends // 2

    def gradients(kernel, tiles, params, begun, out_shape, scratch, share):
        xin, base, slots, counts = tiles
        return pl.pallas_call(
            functools.partial(kernel, sends),
            out_shape=out_shape,
            in_specs=[SMEM] * 2 + [VMEM] * (3 + len(begun)),
            out_specs=jax.tree.map(lambda _: VMEM, out_shape),
            scratch_shapes=scratch,
            compiler_params=PARAMS,
            cost_estimate=pl.CostEstimate(
                flops=int(work * 32 * share), bytes_accessed=1 << 21, transcendentals=1 << 20
            ),
        )(slots, counts, xin, base, params, *begun)

    folded = jax.ShapeDtypeStruct((half,) + params.shape, F32)
    totals = (2 * half, 256, 128)
    tiles = tiles_0
    for snapshot in range(SNAPS):
        far, begun = gradients(
            first_gradient_kernel, tiles, params, [], (folded, jax.ShapeDtypeStruct(totals, F32)), [], 0.75
        )
        arrived = swap(far, "solver", half)
        near = gradients(
            second_gradient_kernel, tiles, params, [begun], folded, [pltpu.VMEM(totals, F32)], 0.5
        )
        near = near + arrived
        if snapshot == 0:
            near, fields, strip = lax.optimization_barrier((near, fields, strip))
            final, *tiles = second_part(fields, strip)
        bit = 1
        while 2 * bit < half:
            near = near + swap(near, "solver", bit)
            bit = 2 * bit
            if snapshot == 0:
                near, *tiles = lax.optimization_barrier((near, *tiles))
        direction = pl.pallas_call(
            functools.partial(combine_kernel, entries),
            out_shape=jax.ShapeDtypeStruct(params.shape, F32),
            in_specs=[VMEM] * 2,
            out_specs=VMEM,
            compiler_params=PARAMS,
        )(near, swap(near, "solver", bit))
        across = [(i, i ^ (half * trainers + 1)) for i in range(solvers * trainers)]
        direction = direction + lax.ppermute(direction, ("solver", "trainer"), across)
        direction = direction + swap(direction, "trainer", 1)
        direction = direction / (solvers * trainers)
        change = change + direction
        params = params - STEP_RATE * direction
    first, mix, last = unpack_weights(change)
    return (final, first, mix, last)


def solution(mesh):
    return jax.shard_map(
        local,
        mesh=mesh,
        in_specs=(
            P(("groups", "solver"), "trainer"),
            P(("groups", "solver"), "trainer"),
            P("groups"),
            P("groups", None),
            P("groups", "solver", "trainer", None),
            P("groups", "solver", "trainer", None, None),
            P("groups", None, None),
            P("groups", None),
            P("groups", None, None),
        ),
        out_specs=(
            P(("groups", "solver"), "trainer"),
            P("groups", None, None),
            P("groups", None),
            P("groups", None, None),
        ),
        check_vma=False,
    )
```

```python
import functools

import jax
import jax.numpy as jnp
from jax import lax
from jax.experimental import pallas as pl
from jax.experimental.pallas import tpu as pltpu
from jax.sharding import PartitionSpec as P

TR = 4
TW = 128
SNAPS = 2
STEPS = 4
EXT = 128
LIVE = 64
BATCH = 8
FIRST = 2

F32 = jnp.float32
BF16 = jnp.bfloat16
STEP_RATE = 0.05
NORM_EPS = 1e-06
GELU_A = 0.7978845608028654
GELU_B = 0.044715

VMEM = pl.BlockSpec(memory_space=pltpu.VMEM)
SMEM = pl.BlockSpec(memory_space=pltpu.SMEM)
PARAMS = pltpu.CompilerParams(vmem_limit_bytes=24 * 1024 * 1024)


def look_up(tables, which, out):
    rows = [jnp.broadcast_to(tables[k : k + 1, :], (8, 128)) for k in range(4)]
    for c in range(which.shape[1] // 128):
        for r in range(which.shape[0] // 8):
            here = (slice(8 * r, 8 * r + 8), slice(128 * c, 128 * c + 128))
            for k in range(4):
                out[(k,) + here] = jnp.take_along_axis(rows[k], which[here], axis=1)


def advance(read, coef, write, tall, columns):
    lane = lax.broadcasted_iota(jnp.int32, (tall, 128), 1)
    cut = [slice(128 * c, 128 * c + 128) for c in range(columns)]
    before = pltpu.roll(read(cut[-1]), 1, 1)
    first = pltpu.roll(read(cut[0]), 127, 1)
    ahead = first
    for c in range(columns):
        center = read(cut[c])
        own = pltpu.roll(center, 1, 1)
        left = jnp.where(lane == 0, before, own)
        following = pltpu.roll(read(cut[c + 1]), 127, 1) if c + 1 < columns else first
        right = jnp.where(lane == 127, following, ahead)
        before, ahead = own, following
        up = pltpu.roll(center, 1, 0)
        down = pltpu.roll(center, tall - 1, 0)
        write(
            cut[c],
            center
            + coef(0, cut[c]) * (up - center)
            + coef(1, cut[c]) * (down - center)
            + coef(2, cut[c]) * (left - center)
            + coef(3, cut[c]) * (right - center),
        )


def inner_kernel(both, ext, tables, fields, coef, ids, start):
    rows, lanes = both.shape[1:]
    wide = lanes + EXT
    ids[:, 0:lanes] = both[1].astype(jnp.int32)
    ids[:, lanes:wide] = ext[1].astype(jnp.int32)
    start[:, 0:lanes] = both[0]
    start[:, lanes:wide] = ext[0]
    look_up(tables, ids, coef)
    for step in range(STEPS):
        source = start if step == 0 else fields.at[step - 1]
        target = fields.at[step]

        def write(cut, new):
            target[:, cut] = new

        advance(lambda cut: source[:, cut], lambda k, cut: coef[k, :, cut], write, rows, wide // 128)


def spare_slots(sends):
    return -sends % BATCH


def pick_tiles(snapshot, sizes, place, tile_pos, tile_dest, both, main, strip, tables, xin, base, slots):
    sends, per_row, half, blocks = sizes
    mine = lax.div(place[0], half)
    sub = lax.broadcasted_iota(jnp.int32, (8, 128), 0)
    channel = tables[8:16]
    aways = [(lax.div(tile_dest[snapshot, k], half) != mine).astype(jnp.int32) for k in range(sends)]
    slots[sends + spare_slots(sends)] = sum(aways)
    far, near = jnp.int32(0), sum(aways)
    for k in range(sends):
        away = aways[k]
        slot = jnp.where(away == 1, far, near)
        far, near = far + away, near + 1 - away
        slots[slot] = lax.rem(tile_dest[snapshot, k], half) + half * (1 - away)
        where = tile_pos[snapshot, k]
        block = lax.div(where, per_row)
        lanes = pl.ds(pl.multiple_of(lax.rem(where, per_row) * TW, TW), TW)
        group = pl.ds(pl.multiple_of(lax.div(block, 2) * 8, 8), 8)
        edge = (block == 0) | (block == blocks - 1)
        beside = pl.ds(pl.multiple_of(jnp.where(block == 0, 16, 0), 8), 8)
        lower = lax.rem(block, 2) == 1

        def tile(x):
            return jnp.where(lower, pltpu.roll(x, TR, 0), x)

        def value(at):
            return tile(jnp.where(edge, strip[at][beside, lanes], main[at][group, lanes]))

        old = value(0)
        which = tile(both[1, group, lanes]).astype(jnp.int32)
        base[slot] = (old - value(1))[0:TR]
        for r in range(TR):
            found = jnp.take_along_axis(channel, jnp.broadcast_to(which[r : r + 1], (8, 128)), axis=1)
            xin[slot, r] = jnp.where(sub % 4 == 0, jnp.broadcast_to(old[r : r + 1], (8, 128)), found)


def strip_coef(coef, outer, rows):
    return lambda k, cut: jnp.concatenate(
        [coef[k, rows - 8 : rows, cut], outer[k, :, cut], coef[k, 0:8, cut]], axis=0
    )


def first_strip_kernel(
    sizes, place, tile_pos, tile_dest, both, ext, first, second, tables, coef, fields, xin, base, slots, strip, outer, ids, work,
):
    rows, lanes = both.shape[1:]
    wide = lanes + EXT
    odd = lax.rem(place[0], 2) == 1
    above = jnp.where(odd, first[...], second[...])
    below = jnp.where(odd, second[...], first[...])
    none = jnp.zeros((2, wide), F32)
    ids[...] = jnp.concatenate([below[STEPS:], none, above[STEPS:]], axis=0).astype(jnp.int32)
    look_up(tables, ids, outer)
    work[0, 0:8, 0:lanes] = both[0, rows - 8 : rows]
    work[0, 0:8, lanes:wide] = ext[0, rows - 8 : rows]
    work[0, 8:16] = jnp.concatenate([below[:STEPS], above[:STEPS]], axis=0)
    work[0, 16:24, 0:lanes] = both[0, 0:8]
    work[0, 16:24, lanes:wide] = ext[0, 0:8]
    for step in range(2):
        source = work.at[step]
        target = work.at[1] if step == 0 else strip

        def write(cut, new):
            target[:, cut] = new

        advance(lambda cut: source[:, cut], strip_coef(coef, outer, rows), write, 24, wide // 128)
    pick_tiles(
        0, sizes, place, tile_pos, tile_dest, both, (fields.at[0], fields.at[1]), (work.at[1], strip),
        tables, xin, base, slots,
    )


def second_strip_kernel(
    sizes, place, tile_pos, tile_dest, both, tables, coef, fields, strip, outer, final, xin, base, slots, work,
):
    rows, lanes = both.shape[1:]
    wide = lanes + EXT
    for step in range(2):
        source = strip if step == 0 else work.at[0]
        target = work.at[step]

        def write(cut, new):
            target[:, cut] = new

        advance(lambda cut: source[:, cut], strip_coef(coef, outer, rows), write, 24, wide // 128)
    sub = lax.broadcasted_iota(jnp.int32, (8, lanes), 0)
    final[0:8] = jnp.where(sub < STEPS, work[1, 16:24, 0:lanes], fields[3, 0:8, 0:lanes])
    final[8 : rows - 8] = fields[3, 8 : rows - 8, 0:lanes]
    final[rows - 8 : rows] = jnp.where(sub >= 8 - STEPS, work[1, 0:8, 0:lanes], fields[3, rows - 8 : rows, 0:lanes])
    pick_tiles(
        1, sizes, place, tile_pos, tile_dest, both, (fields.at[2], fields.at[3]), (work.at[0], work.at[1]),
        tables, xin, base, slots,
    )


def split(x):
    high = x.astype(BF16)
    return high, (x - high.astype(F32)).astype(BF16)


def weights3(w):
    high = w.astype(BF16).astype(F32)
    return jnp.concatenate([high, high, w - high], axis=1).astype(BF16)


def values3(high, low):
    return jnp.concatenate([high, low, high], axis=0)


def times(a, b):
    return lax.dot_general(a, b, (((1,), (0,)), ((), ())), preferred_element_type=F32)


def over_cells(a, b):
    return lax.dot_general(a, b, (((1,), (1,)), ((), ())), preferred_element_type=F32)


def gelu_and_slope(z):
    square = z * z
    t = jnp.tanh(z * (GELU_A + (GELU_A * GELU_B) * square))
    gate = 0.5 + 0.5 * t
    value = z * gate
    return value, gate + (value - value * gate) * (2 * GELU_A + (6 * GELU_A * GELU_B) * square)


def lane_shift(x, by):
    lane = lax.broadcasted_iota(jnp.int32, x.shape, 1)
    return jnp.where(lane == (0 if by == 1 else TW - 1), 0.0, pltpu.roll(x, by % TW, 1))


def batch_gradients(cells, gaps, weights):
    w1, mix, w3, w3_t, mix_t = weights
    number = len(cells)
    zero8 = jnp.zeros((8, TW), F32)
    sub8 = lax.broadcasted_iota(jnp.int32, (8, TW), 0)
    columns = []
    for tile in cells:
        sides = [jnp.where(sub8 < 4, lane_shift(x, 1), lane_shift(x, -1)) for x in tile]
        sides = [zero8] + sides + [zero8]
        center = [zero8] + list(tile) + [zero8]
        for r in range(TR):
            stacked = []
            for dr in range(3):
                stacked += [sides[r + dr], center[r + dr]]
            columns.append(jnp.concatenate(stacked, axis=0))
    x_hi, x_lo = split(jnp.concatenate(columns, axis=1))
    h1, slope1 = gelu_and_slope(times(w1, values3(x_hi, x_lo)))
    h1_hi, h1_lo = split(h1)
    h2, slope2 = gelu_and_slope(times(mix, values3(h1_hi, h1_lo)))
    h2_hi, h2_lo = split(h2)
    taps = times(w3, values3(h2_hi, h2_lo))

    sub = lax.broadcasted_iota(jnp.int32, (16, TW), 0)
    tap_col, tap_row = lax.rem(sub, 3), lax.div(sub, 3)
    zero16 = jnp.zeros((16, TW), F32)

    def by_col(x, by):
        return jnp.where(
            tap_col == 0, lane_shift(x, by), jnp.where(tap_col == 2, lane_shift(x, -by), x)
        )

    def by_row(first, middle, last):
        return jnp.where(
            tap_row == 0, first, jnp.where(tap_row == 1, middle, jnp.where(tap_row == 2, last, 0.0))
        )

    spread = []
    for t in range(number):
        moved = [zero16]
        for r in range(TR):
            at = (t * TR + r) * TW
            moved.append(by_col(taps[:, at : at + TW], 1))
        moved.append(zero16)
        errors = [zero16]
        for r in range(TR):
            summed = jnp.sum(by_row(moved[r], moved[r + 1], moved[r + 2]), axis=0, keepdims=True)
            errors.append(by_col(jnp.broadcast_to(2.0 * (summed + gaps[t][r]), (16, TW)), -1))
        errors.append(zero16)
        spread += [by_row(errors[r + 2], errors[r + 1], errors[r]) for r in range(TR)]
    e_hi, e_lo = split(jnp.concatenate(spread, axis=1))
    d2_hi, d2_lo = split(times(w3_t, values3(e_hi, e_lo)) * slope2)
    d1_hi, d1_lo = split(times(mix_t, values3(d2_hi, d2_lo)) * slope1)

    result = []
    for t in range(number):
        own = slice(t * TR * TW, (t + 1) * TR * TW)
        both = lambda high, low: jnp.concatenate([high[:, own], low[:, own]], axis=0)
        result.append(
            jnp.concatenate(
                [
                    over_cells(both(d2_hi, d2_lo), both(h1_hi, h1_lo)),
                    over_cells(both(x_hi, x_lo), both(d1_hi, d1_lo)),
                    over_cells(both(e_hi, e_lo), both(h2_hi, h2_lo)),
                ],
                axis=0,
            )
        )
    return result


def add_batches(first, last, sends, slots, xin, base, params, total):
    mix = jnp.concatenate([params[0:32, 0:64], params[0:32, 64:128]], axis=0)
    side, rest = params[32:56, 0:64], params[32:56, 64:128]
    none = jnp.zeros((8, 64), F32)
    taps = [[side[8 * r : 8 * r + 8], rest[4 * r : 4 * r + 4], none[0:4]] for r in range(3)]
    w1 = jnp.concatenate(sum(taps, []), axis=0)
    w3 = jnp.concatenate([rest[12:21], none[0:7]], axis=0)
    weights = (weights3(w1.T), weights3(mix), weights3(w3), weights3(w3.T), weights3(mix.T))

    def body(i, carry):
        at = [i * BATCH + k for k in range(BATCH)]
        cells = [[xin[j, r] for r in range(TR)] for j in at]
        gaps = [[base[j, r : r + 1, :] for r in range(TR)] for j in at]
        into = [slots[j] for j in at]
        if sends % BATCH:
            cells = [[jnp.where(j < sends, x, 0.0) for x in tile] for j, tile in zip(at, cells)]
            gaps = [[jnp.where(j < sends, x, 0.0) for x in tile] for j, tile in zip(at, gaps)]
            into = [jnp.where(j < sends, slot, 0) for j, slot in zip(at, into)]
        for buffer, grad in zip(into, batch_gradients(cells, gaps, weights)):
            total[buffer] += grad
        return carry

    lax.fori_loop(first, last, body, 0)


def fold(sums):
    def parts(first, height):
        x = sums[first : first + height, :] + sums[first + height : first + 2 * height, :]
        return x[:, 0:64] + x[:, 64:128]

    d_mix, d_w1, d_w3 = parts(0, 64), parts(128, 48), parts(224, 16)
    side = [d_w1[16 * r : 16 * r + 8] for r in range(3)]
    center = [d_w1[16 * r + 8 : 16 * r + 12] for r in range(3)]
    rest = jnp.concatenate(center + [d_w3[0:9], jnp.zeros((3, 64), F32)], axis=0)
    return jnp.concatenate(
        [
            jnp.concatenate([d_mix[0:32], d_mix[32:64]], axis=1),
            jnp.concatenate([jnp.concatenate(side, axis=0), rest], axis=1),
        ],
        axis=0,
    )


def batches_in_first(far, sends):
    return jnp.maximum(lax.div(far + (BATCH - 1), BATCH), FIRST * -(-sends // BATCH) // 3)


def first_gradient_kernel(sends, slots, xin, base, params, far, total):
    half = far.shape[0]
    total[...] = jnp.zeros_like(total)
    add_batches(0, batches_in_first(slots[sends + spare_slots(sends)], sends), sends, slots, xin, base, params, total)
    for b in range(half):
        far[b] = fold(total.at[b])


def second_gradient_kernel(sends, slots, xin, base, params, begun, near, total):
    half = near.shape[0]
    total[half : 2 * half] = begun[half : 2 * half]
    last = -(-sends // BATCH)
    add_batches(batches_in_first(slots[sends + spare_slots(sends)], sends), last, sends, slots, xin, base, params, total)
    for b in range(half):
        near[b] = fold(total.at[half + b])


def combine_kernel(entries, own, other, out):
    result = jnp.zeros(out.shape, F32)
    for b in range(own.shape[0]):
        full = own[b] + other[b]
        square = jnp.sum(full * full, keepdims=True)
        result = result + full * lax.rsqrt(square / entries + NORM_EPS)
    out[...] = result


def pack_weights(conv_in, mix_weight, conv_out):
    taps = jnp.transpose(conv_in, (0, 2, 1)).reshape(3, 3, 4, conv_in.shape[1])
    side = jnp.concatenate([taps[:, 0], taps[:, 2]], axis=1).reshape(24, conv_in.shape[1])
    rest = jnp.concatenate(
        [taps[:, 1].reshape(12, conv_in.shape[1]), jnp.pad(conv_out[:, 0, :], ((0, 3), (0, 0)))], axis=0
    )
    mix = jnp.concatenate([mix_weight[0:32], mix_weight[32:64]], axis=1)
    return jnp.concatenate([mix, jnp.concatenate([side, rest], axis=1)], axis=0)


def unpack_kernel(one, other, conv_in, mix, conv_out):
    mix_rows = mix.shape[0] // 2
    for k in range(2):
        at = slice(64 * k, 64 * k + 64)
        mix[mix_rows * k : mix_rows * (k + 1)] = one[0:mix_rows, at] + other[0:mix_rows, at]
    side = one[32:56, 0:64] + other[32:56, 0:64]
    rest = one[32:56, 64:128] + other[32:56, 64:128]
    for r in range(3):
        conv_in[3 * r] = side[8 * r : 8 * r + 4]
        conv_in[3 * r + 1] = rest[4 * r : 4 * r + 4]
        conv_in[3 * r + 2] = side[8 * r + 4 : 8 * r + 8]
    for k in range(9):
        conv_out[k] = rest[12 + k : 13 + k]


def local(
    initial_field,
    coef_index,
    kappa_table,
    drift_table,
    tile_pos,
    tile_dest,
    conv_in,
    mix_weight,
    conv_out,
):
    rows, lanes = initial_field.shape
    solvers = lax.axis_size("solver")
    trainers = lax.axis_size("trainer")
    half = solvers // 2
    j = lax.axis_index("solver")
    t = lax.axis_index("trainer")
    sends = tile_pos.shape[-1]
    entries = conv_in.size + mix_weight.size + conv_out.size

    def swap(x, axis, bit):
        count = lax.axis_size(axis)
        return lax.ppermute(x, axis, [(i, i ^ bit) for i in range(count)])

    place = j.reshape(1)
    tile_pos = tile_pos.reshape(SNAPS, sends)
    tile_dest = tile_dest.reshape(SNAPS, sends)
    both = lax.optimization_barrier(jnp.stack([initial_field, (coef_index + 1).astype(F32)]))
    ext = swap(jnp.where(t == 0, both[:, :, lanes - EXT :], both[:, :, :EXT]), "trainer", 1)
    lane = lax.broadcasted_iota(jnp.int32, ext.shape, 2)
    ext = jnp.where((lane < LIVE) == (t == 0), ext, 0.0)

    def edge_rows(bottom):
        def part(k, height):
            start = jnp.where(bottom, rows - height, 0)
            own = lax.dynamic_slice_in_dim(both[k], start, height, 0)
            return jnp.concatenate([own, lax.dynamic_slice_in_dim(ext[k], start, height, 0)], axis=1)

        return jnp.concatenate([part(0, STEPS), part(1, STEPS - 1)], axis=0)

    odd = j % 2 == 1
    inner = [(i, i ^ 1) for i in range(solvers)]
    outer_pairs = [(i, i + 1) for i in range(1, solvers - 1, 2)] + [(i + 1, i) for i in range(1, solvers - 1, 2)]
    first = lax.ppermute(edge_rows(~odd), "solver", inner)
    second = lax.ppermute(edge_rows(odd), "solver", outer_pairs)

    vr, vc = drift_table[0], drift_table[1]
    tables = jnp.stack(
        [
            kappa_table + jnp.maximum(vr, 0.0),
            kappa_table - jnp.minimum(vr, 0.0),
            kappa_table + jnp.maximum(vc, 0.0),
            kappa_table - jnp.minimum(vc, 0.0),
        ]
    )
    none = jnp.zeros_like(kappa_table)
    channel = jnp.stack([none, kappa_table, vr, vc, none, kappa_table, vr, vc])
    fill = 127 - kappa_table.shape[0]
    tables = jnp.pad(jnp.concatenate([tables, jnp.zeros_like(tables), channel]), ((0, 0), (1, fill)))

    sizes = (sends, lanes // TW, half, rows // TR)
    wide = lanes + EXT
    spare = spare_slots(sends)
    tile_shapes = (
        jax.ShapeDtypeStruct((sends + spare, TR, 8, TW), F32),
        jax.ShapeDtypeStruct((sends + spare, TR, TW), F32),
        jax.ShapeDtypeStruct((sends + spare + 1,), jnp.int32),
    )
    tile_specs = (VMEM, VMEM, SMEM)
    fields, coef = pl.pallas_call(
        inner_kernel,
        out_shape=(
            jax.ShapeDtypeStruct((STEPS, rows, wide), F32),
            jax.ShapeDtypeStruct((4, rows, wide), F32),
        ),
        in_specs=[VMEM] * 3,
        out_specs=(VMEM,) * 2,
        scratch_shapes=[pltpu.VMEM((rows, wide), jnp.int32), pltpu.VMEM((rows, wide), F32)],
        compiler_params=PARAMS,
        cost_estimate=pl.CostEstimate(flops=1 << 31, bytes_accessed=1 << 23, transcendentals=0),
    )(both, ext, tables)
    *tiles_0, strip, outer = pl.pallas_call(
        functools.partial(first_strip_kernel, sizes),
        out_shape=tile_shapes
        + (jax.ShapeDtypeStruct((24, wide), F32), jax.ShapeDtypeStruct((4, 8, wide), F32)),
        in_specs=[SMEM] * 3 + [VMEM] * 7,
        out_specs=tile_specs + (VMEM, VMEM),
        scratch_shapes=[pltpu.VMEM((8, wide), jnp.int32), pltpu.VMEM((2, 24, wide), F32)],
        compiler_params=PARAMS,
    )(place, tile_pos, tile_dest, both, ext, first, second, tables, coef, fields)

    def second_part(fields, strip):
        return pl.pallas_call(
            functools.partial(second_strip_kernel, sizes),
            out_shape=(jax.ShapeDtypeStruct((rows, lanes), F32),) + tile_shapes,
            in_specs=[SMEM] * 3 + [VMEM] * 6,
            out_specs=(VMEM,) + tile_specs,
            scratch_shapes=[pltpu.VMEM((2, 24, wide), F32)],
            compiler_params=PARAMS,
            cost_estimate=pl.CostEstimate(flops=1 << 31, bytes_accessed=1 << 23, transcendentals=0),
        )(place, tile_pos, tile_dest, both, tables, coef, fields, strip, outer)

    params = pack_weights(conv_in, mix_weight, conv_out)
    changes = []
    work = 3 * 2 * 20000 * TR * TW * sends // 2

    def gradients(kernel, tiles, params, begun, out_shape, scratch, share):
        xin, base, slots = tiles
        return pl.pallas_call(
            functools.partial(kernel, sends),
            out_shape=out_shape,
            in_specs=[SMEM] + [VMEM] * (3 + len(begun)),
            out_specs=jax.tree.map(lambda _: VMEM, out_shape),
            scratch_shapes=scratch,
            compiler_params=PARAMS,
            cost_estimate=pl.CostEstimate(
                flops=int(work * 32 * share), bytes_accessed=1 << 21, transcendentals=1 << 20
            ),
        )(slots, xin, base, params, *begun)

    folded = jax.ShapeDtypeStruct((half,) + params.shape, F32)
    totals = (2 * half, 256, 128)
    tiles = tiles_0
    for snapshot in range(SNAPS):
        far, begun = gradients(
            first_gradient_kernel, tiles, params, [], (folded, jax.ShapeDtypeStruct(totals, F32)), [], 0.75
        )
        arrived = swap(far, "solver", half)
        near = gradients(
            second_gradient_kernel, tiles, params, [begun], folded, [pltpu.VMEM(totals, F32)], 0.5
        )
        near = near + arrived
        if snapshot == 0:
            near, fields, strip = lax.optimization_barrier((near, fields, strip))
            final, *tiles = second_part(fields, strip)
        bit = 1
        while 2 * bit < half:
            near = near + swap(near, "solver", bit)
            bit = 2 * bit
            if snapshot == 0:
                near, *tiles = lax.optimization_barrier((near, *tiles))
        direction = pl.pallas_call(
            functools.partial(combine_kernel, entries),
            out_shape=jax.ShapeDtypeStruct(params.shape, F32),
            in_specs=[VMEM] * 2,
            out_specs=VMEM,
            compiler_params=PARAMS,
        )(near, swap(near, "solver", bit))
        across = [(i, i ^ (half * trainers + 1)) for i in range(solvers * trainers)]
        direction = direction + lax.ppermute(direction, ("solver", "trainer"), across)
        direction = direction + swap(direction, "trainer", 1)
        direction = direction / (solvers * trainers)
        changes.append(direction)
        params = params - STEP_RATE * direction
    first, mix, last = pl.pallas_call(
        unpack_kernel,
        out_shape=tuple(jax.ShapeDtypeStruct(w.shape, F32) for w in (jnp.transpose(conv_in, (0, 2, 1)), mix_weight, conv_out)),
        in_specs=[VMEM] * 2,
        out_specs=(VMEM,) * 3,
        compiler_params=PARAMS,
    )(*changes)
    return (final, jnp.transpose(first, (0, 2, 1)), mix, last)


def solution(mesh):
    return jax.shard_map(
        local,
        mesh=mesh,
        in_specs=(
            P(("groups", "solver"), "trainer"),
            P(("groups", "solver"), "trainer"),
            P("groups"),
            P("groups", None),
            P("groups", "solver", "trainer", None),
            P("groups", "solver", "trainer", None, None),
            P("groups", None, None),
            P("groups", None),
            P("groups", None, None),
        ),
        out_specs=(
            P(("groups", "solver"), "trainer"),
            P("groups", None, None),
            P("groups", None),
            P("groups", None, None),
        ),
        check_vma=False,
    )
```

```python
import functools

import jax
import jax.numpy as jnp
from jax import lax
from jax.experimental import pallas as pl
from jax.experimental.pallas import tpu as pltpu
from jax.sharding import PartitionSpec as P

TR = 4
TW = 128
SNAPS = 2
STEPS = 4
EXT = 128
LIVE = 64
BATCH = 8

F32 = jnp.float32
BF16 = jnp.bfloat16
STEP_RATE = 0.05
NORM_EPS = 1e-06
GELU_A = 0.7978845608028654
GELU_B = 0.044715

VMEM = pl.BlockSpec(memory_space=pltpu.VMEM)
SMEM = pl.BlockSpec(memory_space=pltpu.SMEM)
PARAMS = pltpu.CompilerParams(vmem_limit_bytes=24 * 1024 * 1024)


def look_up(tables, which, out):
    rows = [jnp.broadcast_to(tables[k : k + 1, :], (8, 128)) for k in range(4)]
    for c in range(which.shape[1] // 128):
        for r in range(which.shape[0] // 8):
            here = (slice(8 * r, 8 * r + 8), slice(128 * c, 128 * c + 128))
            for k in range(4):
                out[(k,) + here] = jnp.take_along_axis(rows[k], which[here], axis=1)


def advance(read, coef, write, tall, columns):
    lane = lax.broadcasted_iota(jnp.int32, (tall, 128), 1)
    cut = [slice(128 * c, 128 * c + 128) for c in range(columns)]
    before = pltpu.roll(read(cut[-1]), 1, 1)
    first = pltpu.roll(read(cut[0]), 127, 1)
    ahead = first
    for c in range(columns):
        center = read(cut[c])
        own = pltpu.roll(center, 1, 1)
        left = jnp.where(lane == 0, before, own)
        following = pltpu.roll(read(cut[c + 1]), 127, 1) if c + 1 < columns else first
        right = jnp.where(lane == 127, following, ahead)
        before, ahead = own, following
        up = pltpu.roll(center, 1, 0)
        down = pltpu.roll(center, tall - 1, 0)
        write(
            cut[c],
            center
            + coef(0, cut[c]) * (up - center)
            + coef(1, cut[c]) * (down - center)
            + coef(2, cut[c]) * (left - center)
            + coef(3, cut[c]) * (right - center),
        )


def inner_kernel(sizes, place, tile_pos, tile_dest, both, ext, tables, fields, coef, xin, base, slots, ids, start):
    order_tiles(0, sizes, True, place, tile_pos, tile_dest, slots)
    rows, lanes = both.shape[1:]
    wide = lanes + EXT
    ids[:, 0:lanes] = both[1].astype(jnp.int32)
    ids[:, lanes:wide] = ext[1].astype(jnp.int32)
    start[:, 0:lanes] = both[0]
    start[:, lanes:wide] = ext[0]
    look_up(tables, ids, coef)
    for step in range(STEPS):
        source = start if step == 0 else fields.at[step - 1]
        target = fields.at[step]

        def write(cut, new):
            target[:, cut] = new

        advance(lambda cut: source[:, cut], lambda k, cut: coef[k, :, cut], write, rows, wide // 128)
    main = (fields.at[0], fields.at[1])
    pick_tiles(0, sizes, True, 0, tile_pos, slots, both.at[1], main, None, tables, xin, base)


def lead_of(early):
    return BATCH if early else 0


def slot_count(sends, early):
    return lead_of(early) - (-sends // BATCH) * BATCH


def order_tiles(snapshot, sizes, early, place, tile_pos, tile_dest, slots):
    sends, per_row, half, blocks = sizes
    total, lead = slot_count(sends, early), lead_of(early)
    mine = lax.div(place[0], half)
    for slot in range(2 * total):
        slots[slot] = 0
    buffers, aways, inners = [], [], []
    for k in range(sends):
        dest = tile_dest[snapshot, k]
        away = (lax.div(dest, half) != mine).astype(jnp.int32)
        block = lax.div(tile_pos[snapshot, k], per_row)
        aways.append(away)
        inners.append(((block != 0) & (block != blocks - 1)).astype(jnp.int32) if early else jnp.int32(0))
        buffers.append(lax.rem(dest, half) + half * (1 - away))
    early_far = jnp.minimum(lead, sum(x * y for x, y in zip(aways, inners)))
    early_near = jnp.minimum(lead - early_far, sum((1 - x) * y for x, y in zip(aways, inners)))
    rest_far = sum(aways) - early_far
    one, two, three, four = jnp.int32(0), jnp.int32(0), jnp.int32(lead), lead + rest_far
    for k in range(sends):
        away, inner = aways[k], inners[k]
        first = away * inner * (one < early_far).astype(jnp.int32)
        second = (1 - away) * inner * (two < early_near).astype(jnp.int32)
        slot = jnp.where(away == 1, jnp.where(first == 1, one, three), jnp.where(second == 1, early_far + two, four))
        one, two = one + first, two + second
        three, four = three + away - first, four + 1 - away - second
        slots[slot] = buffers[k]
        slots[total + slot] = k
    slots[2 * total] = early_far + early_near
    slots[2 * total + 1] = rest_far
    slots[2 * total + 2] = sends - early_far - early_near


def pick_tiles(snapshot, sizes, early, first, tile_pos, slots, numbers, main, strip, tables, xin, base):
    sends, per_row, half, blocks = sizes
    total = slot_count(sends, early)
    sub = lax.broadcasted_iota(jnp.int32, (8, 128), 0)
    channel = tables[8:16]
    for slot in range(xin.shape[0]):
        where = tile_pos[snapshot, slots[total + first + slot]]
        block = lax.div(where, per_row)
        lanes = pl.ds(pl.multiple_of(lax.rem(where, per_row) * TW, TW), TW)
        group = pl.ds(pl.multiple_of(lax.div(block, 2) * 8, 8), 8)
        edge = (block == 0) | (block == blocks - 1)
        beside = pl.ds(pl.multiple_of(jnp.where(block == 0, 16, 0), 8), 8)
        lower = lax.rem(block, 2) == 1

        def tile(x):
            return jnp.where(lower, pltpu.roll(x, TR, 0), x)

        def value(at):
            inside = main[at][group, lanes]
            if strip is None:
                return tile(inside)
            return tile(jnp.where(edge, strip[at][beside, lanes], inside))

        old = value(0)
        which = tile(numbers[group, lanes]).astype(jnp.int32)
        base[slot] = (old - value(1))[0:TR]
        for r in range(TR):
            found = jnp.take_along_axis(channel, jnp.broadcast_to(which[r : r + 1], (8, 128)), axis=1)
            xin[slot, r] = jnp.where(sub % 4 == 0, jnp.broadcast_to(old[r : r + 1], (8, 128)), found)


def strip_coef(coef, outer, rows):
    return lambda k, cut: jnp.concatenate(
        [coef[k, rows - 8 : rows, cut], outer[k, :, cut], coef[k, 0:8, cut]], axis=0
    )


def first_strip_kernel(
    sizes, place, tile_pos, slots, both, ext, first, second, tables, coef, fields, xin, base, strip, outer, ids, work,
):
    rows, lanes = both.shape[1:]
    wide = lanes + EXT
    odd = lax.rem(place[0], 2) == 1
    above = jnp.where(odd, first[...], second[...])
    below = jnp.where(odd, second[...], first[...])
    none = jnp.zeros((2, wide), F32)
    ids[...] = jnp.concatenate([below[STEPS:], none, above[STEPS:]], axis=0).astype(jnp.int32)
    look_up(tables, ids, outer)
    work[0, 0:8, 0:lanes] = both[0, rows - 8 : rows]
    work[0, 0:8, lanes:wide] = ext[0, rows - 8 : rows]
    work[0, 8:16] = jnp.concatenate([below[:STEPS], above[:STEPS]], axis=0)
    work[0, 16:24, 0:lanes] = both[0, 0:8]
    work[0, 16:24, lanes:wide] = ext[0, 0:8]
    for step in range(2):
        source = work.at[step]
        target = work.at[1] if step == 0 else strip

        def write(cut, new):
            target[:, cut] = new

        advance(lambda cut: source[:, cut], strip_coef(coef, outer, rows), write, 24, wide // 128)
    main = (fields.at[0], fields.at[1])
    edge = (work.at[1], strip)
    pick_tiles(0, sizes, True, BATCH, tile_pos, slots, both.at[1], main, edge, tables, xin, base)


def second_strip_kernel(
    sizes, place, tile_pos, tile_dest, both, tables, coef, fields, strip, outer, final, xin, base, slots, work,
):
    rows, lanes = both.shape[1:]
    wide = lanes + EXT
    for step in range(2):
        source = strip if step == 0 else work.at[0]
        target = work.at[step]

        def write(cut, new):
            target[:, cut] = new

        advance(lambda cut: source[:, cut], strip_coef(coef, outer, rows), write, 24, wide // 128)
    sub = lax.broadcasted_iota(jnp.int32, (8, lanes), 0)
    final[0:8] = jnp.where(sub < STEPS, work[1, 16:24, 0:lanes], fields[3, 0:8, 0:lanes])
    final[8 : rows - 8] = fields[3, 8 : rows - 8, 0:lanes]
    final[rows - 8 : rows] = jnp.where(sub >= 8 - STEPS, work[1, 0:8, 0:lanes], fields[3, rows - 8 : rows, 0:lanes])
    order_tiles(1, sizes, False, place, tile_pos, tile_dest, slots)
    main = (fields.at[2], fields.at[3])
    edge = (work.at[0], work.at[1])
    pick_tiles(1, sizes, False, 0, tile_pos, slots, both.at[1], main, edge, tables, xin, base)


def split(x):
    high = x.astype(BF16)
    return high, (x - high.astype(F32)).astype(BF16)


def weights3(w):
    high = w.astype(BF16).astype(F32)
    return jnp.concatenate([high, high, w - high], axis=1).astype(BF16)


def values3(high, low):
    return jnp.concatenate([high, low, high], axis=0)


def times(a, b):
    return lax.dot_general(a, b, (((1,), (0,)), ((), ())), preferred_element_type=F32)


def over_cells(a, b):
    return lax.dot_general(a, b, (((1,), (1,)), ((), ())), preferred_element_type=F32)


def gelu_and_slope(z):
    square = z * z
    t = jnp.tanh(z * (GELU_A + (GELU_A * GELU_B) * square))
    gate = 0.5 + 0.5 * t
    value = z * gate
    return value, gate + (value - value * gate) * (2 * GELU_A + (6 * GELU_A * GELU_B) * square)


def lane_shift(x, by):
    lane = lax.broadcasted_iota(jnp.int32, x.shape, 1)
    return jnp.where(lane == (0 if by == 1 else TW - 1), 0.0, pltpu.roll(x, by % TW, 1))


def batch_gradients(cells, gaps, weights):
    w1, mix, w3, w3_t, mix_t = weights
    number = len(cells)
    zero8 = jnp.zeros((8, TW), F32)
    sub8 = lax.broadcasted_iota(jnp.int32, (8, TW), 0)
    columns = []
    for tile in cells:
        sides = [jnp.where(sub8 < 4, lane_shift(x, 1), lane_shift(x, -1)) for x in tile]
        sides = [zero8] + sides + [zero8]
        center = [zero8] + list(tile) + [zero8]
        for r in range(TR):
            stacked = []
            for dr in range(3):
                stacked += [sides[r + dr], center[r + dr]]
            columns.append(jnp.concatenate(stacked, axis=0))
    x_hi, x_lo = split(jnp.concatenate(columns, axis=1))
    h1, slope1 = gelu_and_slope(times(w1, values3(x_hi, x_lo)))
    h1_hi, h1_lo = split(h1)
    h2, slope2 = gelu_and_slope(times(mix, values3(h1_hi, h1_lo)))
    h2_hi, h2_lo = split(h2)
    taps = times(w3, values3(h2_hi, h2_lo))

    sub = lax.broadcasted_iota(jnp.int32, (16, TW), 0)
    tap_col, tap_row = lax.rem(sub, 3), lax.div(sub, 3)
    zero16 = jnp.zeros((16, TW), F32)

    def by_col(x, by):
        return jnp.where(
            tap_col == 0, lane_shift(x, by), jnp.where(tap_col == 2, lane_shift(x, -by), x)
        )

    def by_row(first, middle, last):
        return jnp.where(
            tap_row == 0, first, jnp.where(tap_row == 1, middle, jnp.where(tap_row == 2, last, 0.0))
        )

    spread = []
    for t in range(number):
        moved = [zero16]
        for r in range(TR):
            at = (t * TR + r) * TW
            moved.append(by_col(taps[:, at : at + TW], 1))
        moved.append(zero16)
        errors = [zero16]
        for r in range(TR):
            summed = jnp.sum(by_row(moved[r], moved[r + 1], moved[r + 2]), axis=0, keepdims=True)
            errors.append(by_col(jnp.broadcast_to(2.0 * (summed + gaps[t][r]), (16, TW)), -1))
        errors.append(zero16)
        spread += [by_row(errors[r + 2], errors[r + 1], errors[r]) for r in range(TR)]
    e_hi, e_lo = split(jnp.concatenate(spread, axis=1))
    d2_hi, d2_lo = split(times(w3_t, values3(e_hi, e_lo)) * slope2)
    d1_hi, d1_lo = split(times(mix_t, values3(d2_hi, d2_lo)) * slope1)

    result = []
    for t in range(number):
        own = slice(t * TR * TW, (t + 1) * TR * TW)
        both = lambda high, low: jnp.concatenate([high[:, own], low[:, own]], axis=0)
        result.append(
            jnp.concatenate(
                [
                    over_cells(both(d2_hi, d2_lo), both(h1_hi, h1_lo)),
                    over_cells(both(x_hi, x_lo), both(d1_hi, d1_lo)),
                    over_cells(both(e_hi, e_lo), both(h2_hi, h2_lo)),
                ],
                axis=0,
            )
        )
    return result


WEIGHTS = ((64, 144), (64, 192), (16, 192), (64, 48), (64, 192))


def prepare(params, weights):
    mix = jnp.concatenate([params[0:32, 0:64], params[0:32, 64:128]], axis=0)
    side, rest = params[32:56, 0:64], params[32:56, 64:128]
    none = jnp.zeros((8, 64), F32)
    taps = [[side[8 * r : 8 * r + 8], rest[4 * r : 4 * r + 4], none[0:4]] for r in range(3)]
    w1 = jnp.concatenate(sum(taps, []), axis=0)
    w3 = jnp.concatenate([rest[12:21], none[0:7]], axis=0)
    for ref, w in zip(weights, (w1.T, mix, w3, w3.T, mix.T)):
        ref[...] = weights3(w)


def add_batches(first, last, lead, number, masked, slots, xin, base, weights, total):
    weights = [ref[...] for ref in weights]

    def body(i, carry):
        at = [i * BATCH + k for k in range(BATCH)]
        cells = [[xin[j, r] for r in range(TR)] for j in at]
        gaps = [[base[j, r : r + 1, :] for r in range(TR)] for j in at]
        into = [slots[lead + j] for j in at]
        if masked:
            cells = [[jnp.where(j < number, x, 0.0) for x in tile] for j, tile in zip(at, cells)]
            gaps = [[jnp.where(j < number, x, 0.0) for x in tile] for j, tile in zip(at, gaps)]
        for buffer, grad in zip(into, batch_gradients(cells, gaps, weights)):
            total[buffer] += grad
        return carry

    lax.fori_loop(first, last, body, 0)


def fold(sums):
    def parts(first, height):
        x = sums[first : first + height, :] + sums[first + height : first + 2 * height, :]
        return x[:, 0:64] + x[:, 64:128]

    d_mix, d_w1, d_w3 = parts(0, 64), parts(128, 48), parts(224, 16)
    side = [d_w1[16 * r : 16 * r + 8] for r in range(3)]
    center = [d_w1[16 * r + 8 : 16 * r + 12] for r in range(3)]
    rest = jnp.concatenate(center + [d_w3[0:9], jnp.zeros((3, 64), F32)], axis=0)
    return jnp.concatenate(
        [
            jnp.concatenate([d_mix[0:32], d_mix[32:64]], axis=1),
            jnp.concatenate([jnp.concatenate(side, axis=0), rest], axis=1),
        ],
        axis=0,
    )


def batches(sends, early, slots):
    at = 2 * slot_count(sends, early)
    rest_far, rest = slots[at + 1], slots[at + 2]
    every = lax.div(rest + (BATCH - 1), BATCH)
    return jnp.maximum(lax.div(rest_far + (BATCH - 1), BATCH), every - 1), every, rest


def first_gradients(sends, early, slots, xin, base, weights, far, total):
    count, every, number = batches(sends, early, slots)
    masked = early or sends % BATCH != 0
    add_batches(0, count, lead_of(early), number, masked, slots, xin, base, weights, total)
    for b in range(far.shape[0]):
        far[b] = fold(total.at[b])


def first_gradient_kernel(sends, slots, xin, base, params, far, total, *weights):
    prepare(params, weights)
    total[...] = jnp.zeros_like(total)
    first_gradients(sends, False, slots, xin, base, weights, far, total)


def second_gradient_kernel(sends, early, slots, xin, base, begun, *rest):
    *weights, near, total = rest
    half = near.shape[0]
    total[half : 2 * half] = begun[half : 2 * half]
    count, every, number = batches(sends, early, slots)
    masked = early or sends % BATCH != 0
    add_batches(count, every, lead_of(early), number, masked, slots, xin, base, weights, total)
    for b in range(half):
        near[b] = fold(total.at[half + b])


def opening_kernel(sizes, place, tile_pos, tile_dest, both, ext, tables, params, fields, coef, slots, begun, *rest):
    *weights, xin, base, ids, start = rest
    prepare(params, weights)
    inner_kernel(sizes, place, tile_pos, tile_dest, both, ext, tables, fields, coef, xin, base, slots, ids, start)
    begun[...] = jnp.zeros_like(begun)
    number = slots[2 * slot_count(sizes[0], True)]
    add_batches(0, jnp.minimum(number, 1), 0, number, True, slots, xin, base, weights, begun)


def edge_kernel(sizes, place, tile_pos, slots, both, ext, first, second, tables, coef, fields, begun, *rest):
    *weights, xin, base, strip, outer, far, total, ids, work = rest
    first_strip_kernel(
        sizes, place, tile_pos, slots, both, ext, first, second, tables, coef, fields, xin, base, strip, outer, ids, work
    )
    total[...] = begun[...]
    first_gradients(sizes[0], True, slots, xin, base, weights, far, total)


def combine_kernel(entries, own, other, out):
    result = jnp.zeros(out.shape, F32)
    for b in range(own.shape[0]):
        full = own[b] + other[b]
        square = jnp.sum(full * full, keepdims=True)
        result = result + full * lax.rsqrt(square / entries + NORM_EPS)
    out[...] = result


def pack_weights(conv_in, mix_weight, conv_out):
    taps = jnp.transpose(conv_in, (0, 2, 1)).reshape(3, 3, 4, conv_in.shape[1])
    side = jnp.concatenate([taps[:, 0], taps[:, 2]], axis=1).reshape(24, conv_in.shape[1])
    rest = jnp.concatenate(
        [taps[:, 1].reshape(12, conv_in.shape[1]), jnp.pad(conv_out[:, 0, :], ((0, 3), (0, 0)))], axis=0
    )
    mix = jnp.concatenate([mix_weight[0:32], mix_weight[32:64]], axis=1)
    return jnp.concatenate([mix, jnp.concatenate([side, rest], axis=1)], axis=0)


def unpack_kernel(one, other, conv_in, mix, conv_out):
    mix_rows = mix.shape[0] // 2
    for k in range(2):
        at = slice(64 * k, 64 * k + 64)
        mix[mix_rows * k : mix_rows * (k + 1)] = one[0:mix_rows, at] + other[0:mix_rows, at]
    side = one[32:56, 0:64] + other[32:56, 0:64]
    rest = one[32:56, 64:128] + other[32:56, 64:128]
    for r in range(3):
        conv_in[3 * r] = side[8 * r : 8 * r + 4]
        conv_in[3 * r + 1] = rest[4 * r : 4 * r + 4]
        conv_in[3 * r + 2] = side[8 * r + 4 : 8 * r + 8]
    for k in range(9):
        conv_out[k] = rest[12 + k : 13 + k]


def local(
    initial_field,
    coef_index,
    kappa_table,
    drift_table,
    tile_pos,
    tile_dest,
    conv_in,
    mix_weight,
    conv_out,
):
    rows, lanes = initial_field.shape
    solvers = lax.axis_size("solver")
    trainers = lax.axis_size("trainer")
    half = solvers // 2
    j = lax.axis_index("solver")
    t = lax.axis_index("trainer")
    sends = tile_pos.shape[-1]
    entries = conv_in.size + mix_weight.size + conv_out.size

    def swap(x, axis, bit):
        count = lax.axis_size(axis)
        return lax.ppermute(x, axis, [(i, i ^ bit) for i in range(count)])

    place = j.reshape(1)
    tile_pos = tile_pos.reshape(SNAPS, sends)
    tile_dest = tile_dest.reshape(SNAPS, sends)
    both = lax.optimization_barrier(jnp.stack([initial_field, (coef_index + 1).astype(F32)]))
    ext = swap(jnp.where(t == 0, both[:, :, lanes - EXT :], both[:, :, :EXT]), "trainer", 1)
    lane = lax.broadcasted_iota(jnp.int32, ext.shape, 2)
    ext = jnp.where((lane < LIVE) == (t == 0), ext, 0.0)

    def edge_rows(bottom):
        def part(k, height):
            start = jnp.where(bottom, rows - height, 0)
            own = lax.dynamic_slice_in_dim(both[k], start, height, 0)
            return jnp.concatenate([own, lax.dynamic_slice_in_dim(ext[k], start, height, 0)], axis=1)

        return jnp.concatenate([part(0, STEPS), part(1, STEPS - 1)], axis=0)

    odd = j % 2 == 1
    inner = [(i, i ^ 1) for i in range(solvers)]
    outer_pairs = [(i, (i + 1 if i % 2 else i - 1) % solvers) for i in range(solvers)]
    first = lax.ppermute(edge_rows(~odd), "solver", inner)
    second = lax.ppermute(edge_rows(odd), "solver", outer_pairs)
    second = jnp.where((j == 0) | (j == solvers - 1), 0.0, second)

    vr, vc = drift_table[0], drift_table[1]
    tables = jnp.stack(
        [
            kappa_table + jnp.maximum(vr, 0.0),
            kappa_table - jnp.minimum(vr, 0.0),
            kappa_table + jnp.maximum(vc, 0.0),
            kappa_table - jnp.minimum(vc, 0.0),
        ]
    )
    none = jnp.zeros_like(kappa_table)
    channel = jnp.stack([none, kappa_table, vr, vc, none, kappa_table, vr, vc])
    fill = 127 - kappa_table.shape[0]
    tables = jnp.pad(jnp.concatenate([tables, jnp.zeros_like(tables), channel]), ((0, 0), (1, fill)))

    sizes = (sends, lanes // TW, half, rows // TR)
    wide = lanes + EXT
    def tile_shapes(number):
        return (
            jax.ShapeDtypeStruct((number, TR, 8, TW), F32),
            jax.ShapeDtypeStruct((number, TR, TW), F32),
        )

    def slots_shape(early):
        return jax.ShapeDtypeStruct((2 * slot_count(sends, early) + 3,), jnp.int32)

    held = slot_count(sends, False)
    params = pack_weights(conv_in, mix_weight, conv_out)
    changes = []
    work = 3 * 2 * 20000 * TR * TW * sends // 2
    folded = jax.ShapeDtypeStruct((half,) + params.shape, F32)
    totals = jax.ShapeDtypeStruct((2 * half, 256, 128), F32)

    prepared = tuple(jax.ShapeDtypeStruct(shape, BF16) for shape in WEIGHTS)

    def room(shape):
        return pltpu.VMEM(shape.shape, shape.dtype)

    fields, coef, slots, begun, *weights = pl.pallas_call(
        functools.partial(opening_kernel, sizes),
        out_shape=(
            jax.ShapeDtypeStruct((STEPS, rows, wide), F32),
            jax.ShapeDtypeStruct((4, rows, wide), F32),
            slots_shape(True),
            totals,
        )
        + prepared,
        in_specs=[SMEM] * 3 + [VMEM] * 4,
        out_specs=(VMEM, VMEM, SMEM, VMEM) + (VMEM,) * len(prepared),
        scratch_shapes=[room(x) for x in tile_shapes(BATCH)]
        + [pltpu.VMEM((rows, wide), jnp.int32), pltpu.VMEM((rows, wide), F32)],
        compiler_params=PARAMS,
        cost_estimate=pl.CostEstimate(flops=1 << 31, bytes_accessed=1 << 23, transcendentals=0),
    )(place, tile_pos, tile_dest, both, ext, tables, params)

    def gradients(kernel, tiles, others, out_shape, scratch):
        xin, base, slots = tiles
        return pl.pallas_call(
            kernel,
            out_shape=out_shape,
            in_specs=[SMEM] + [VMEM] * (2 + len(others)),
            out_specs=jax.tree.map(lambda _: VMEM, out_shape),
            scratch_shapes=scratch,
            compiler_params=PARAMS,
            cost_estimate=pl.CostEstimate(flops=work * 16, bytes_accessed=1 << 21, transcendentals=1 << 20),
        )(slots, xin, base, *others)

    xin, base, strip, outer, far, begun = pl.pallas_call(
        functools.partial(edge_kernel, sizes),
        out_shape=tile_shapes(held)
        + (jax.ShapeDtypeStruct((24, wide), F32), jax.ShapeDtypeStruct((4, 8, wide), F32), folded, totals),
        in_specs=[SMEM] * 3 + [VMEM] * (8 + len(weights)),
        out_specs=(VMEM,) * 6,
        scratch_shapes=[pltpu.VMEM((8, wide), jnp.int32), pltpu.VMEM((2, 24, wide), F32)],
        compiler_params=PARAMS,
    )(place, tile_pos, slots, both, ext, first, second, tables, coef, fields, begun, *weights)

    def second_part(fields, strip):
        return pl.pallas_call(
            functools.partial(second_strip_kernel, sizes),
            out_shape=(jax.ShapeDtypeStruct((rows, lanes), F32),) + tile_shapes(held) + (slots_shape(False),),
            in_specs=[SMEM] * 3 + [VMEM] * 6,
            out_specs=(VMEM,) * 3 + (SMEM,),
            scratch_shapes=[pltpu.VMEM((2, 24, wide), F32)],
            compiler_params=PARAMS,
            cost_estimate=pl.CostEstimate(flops=1 << 31, bytes_accessed=1 << 23, transcendentals=0),
        )(place, tile_pos, tile_dest, both, tables, coef, fields, strip, outer)

    tiles = (xin, base, slots)
    for snapshot in range(SNAPS):
        early = snapshot == 0
        if not early:
            far, begun, *weights = gradients(
                functools.partial(first_gradient_kernel, sends), tiles, [params], (folded, totals) + prepared, []
            )
        arrived = swap(far, "solver", half)
        near = gradients(
            functools.partial(second_gradient_kernel, sends, early), tiles, [begun, *weights], folded, [room(totals)]
        )
        near = near + arrived
        if snapshot == 0:
            near, fields, strip = lax.optimization_barrier((near, fields, strip))
            final, *tiles = second_part(fields, strip)
        bit = 1
        while 2 * bit < half:
            near = near + swap(near, "solver", bit)
            bit = 2 * bit
            if snapshot == 0:
                near, *tiles = lax.optimization_barrier((near, *tiles))
        direction = pl.pallas_call(
            functools.partial(combine_kernel, entries),
            out_shape=jax.ShapeDtypeStruct(params.shape, F32),
            in_specs=[VMEM] * 2,
            out_specs=VMEM,
            compiler_params=PARAMS,
        )(near, swap(near, "solver", bit))
        across = [(i, i ^ (half * trainers + 1)) for i in range(solvers * trainers)]
        direction = direction + lax.ppermute(direction, ("solver", "trainer"), across)
        direction = direction + swap(direction, "trainer", 1)
        direction = direction / (solvers * trainers)
        changes.append(direction)
        params = params - STEP_RATE * direction
    first, mix, last = pl.pallas_call(
        unpack_kernel,
        out_shape=tuple(jax.ShapeDtypeStruct(w.shape, F32) for w in (jnp.transpose(conv_in, (0, 2, 1)), mix_weight, conv_out)),
        in_specs=[VMEM] * 2,
        out_specs=(VMEM,) * 3,
        compiler_params=PARAMS,
    )(*changes)
    return (final, jnp.transpose(first, (0, 2, 1)), mix, last)


def solution(mesh):
    return jax.shard_map(
        local,
        mesh=mesh,
        in_specs=(
            P(("groups", "solver"), "trainer"),
            P(("groups", "solver"), "trainer"),
            P("groups"),
            P("groups", None),
            P("groups", "solver", "trainer", None),
            P("groups", "solver", "trainer", None, None),
            P("groups", None, None),
            P("groups", None),
            P("groups", None, None),
        ),
        out_specs=(
            P(("groups", "solver"), "trainer"),
            P("groups", None, None),
            P("groups", None),
            P("groups", None, None),
        ),
        check_vma=False,
    )
```

```python
import functools

import jax
import jax.numpy as jnp
from jax import lax
from jax.experimental import pallas as pl
from jax.experimental.pallas import tpu as pltpu
from jax.sharding import PartitionSpec as P

TR = 4
TW = 128
SNAPS = 2
STEPS = 4
EXT = 128
LIVE = 64
BATCH = 8

F32 = jnp.float32
BF16 = jnp.bfloat16
STEP_RATE = 0.05
NORM_EPS = 1e-06
GELU_A = 0.7978845608028654
GELU_B = 0.044715

VMEM = pl.BlockSpec(memory_space=pltpu.VMEM)
SMEM = pl.BlockSpec(memory_space=pltpu.SMEM)
PARAMS = pltpu.CompilerParams(vmem_limit_bytes=24 * 1024 * 1024)


def look_up(tables, which, out):
    rows = [jnp.broadcast_to(tables[k : k + 1, :], (8, 128)) for k in range(4)]
    for c in range(which.shape[1] // 128):
        for r in range(which.shape[0] // 8):
            here = (slice(8 * r, 8 * r + 8), slice(128 * c, 128 * c + 128))
            for k in range(4):
                out[(k,) + here] = jnp.take_along_axis(rows[k], which[here], axis=1)


def advance(read, coef, write, tall, columns):
    lane = lax.broadcasted_iota(jnp.int32, (tall, 128), 1)
    cut = [slice(128 * c, 128 * c + 128) for c in range(columns)]
    before = pltpu.roll(read(cut[-1]), 1, 1)
    first = pltpu.roll(read(cut[0]), 127, 1)
    ahead = first
    for c in range(columns):
        center = read(cut[c])
        own = pltpu.roll(center, 1, 1)
        left = jnp.where(lane == 0, before, own)
        following = pltpu.roll(read(cut[c + 1]), 127, 1) if c + 1 < columns else first
        right = jnp.where(lane == 127, following, ahead)
        before, ahead = own, following
        up = pltpu.roll(center, 1, 0)
        down = pltpu.roll(center, tall - 1, 0)
        write(
            cut[c],
            center
            + coef(0, cut[c]) * (up - center)
            + coef(1, cut[c]) * (down - center)
            + coef(2, cut[c]) * (left - center)
            + coef(3, cut[c]) * (right - center),
        )


def inner_kernel(sizes, place, tile_pos, tile_dest, both, ext, tables, fields, coef, xin, base, slots, ids, start):
    order_tiles(0, sizes, True, place, tile_pos, tile_dest, slots)
    rows, lanes = both.shape[1:]
    wide = lanes + EXT
    ids[:, 0:lanes] = both[1].astype(jnp.int32)
    ids[:, lanes:wide] = ext[1].astype(jnp.int32)
    start[:, 0:lanes] = both[0]
    start[:, lanes:wide] = ext[0]
    look_up(tables, ids, coef)
    for step in range(STEPS):
        source = start if step == 0 else fields.at[step - 1]
        target = fields.at[step]

        def write(cut, new):
            target[:, cut] = new

        advance(lambda cut: source[:, cut], lambda k, cut: coef[k, :, cut], write, rows, wide // 128)
    main = (fields.at[0], fields.at[1])
    pick_tiles(0, sizes, True, 0, tile_pos, slots, both.at[1], main, None, tables, xin, base)


def lead_of(early):
    return BATCH if early else 0


def slot_count(sends, early):
    return lead_of(early) - (-sends // BATCH) * BATCH


def order_tiles(snapshot, sizes, early, place, tile_pos, tile_dest, slots):
    sends, per_row, half, blocks = sizes
    total, lead = slot_count(sends, early), lead_of(early)
    mine = lax.div(place[0], half)
    for slot in range(2 * total):
        slots[slot] = 0
    buffers, aways, inners = [], [], []
    for k in range(sends):
        dest = tile_dest[snapshot, k]
        away = (lax.div(dest, half) != mine).astype(jnp.int32)
        block = lax.div(tile_pos[snapshot, k], per_row)
        aways.append(away)
        inners.append(((block != 0) & (block != blocks - 1)).astype(jnp.int32) if early else jnp.int32(0))
        buffers.append(lax.rem(dest, half) + half * (1 - away))
    early_far = jnp.minimum(lead, sum(x * y for x, y in zip(aways, inners)))
    early_near = jnp.minimum(lead - early_far, sum((1 - x) * y for x, y in zip(aways, inners)))
    rest_far = sum(aways) - early_far
    one, two, three, four = jnp.int32(0), jnp.int32(0), jnp.int32(lead), lead + rest_far
    for k in range(sends):
        away, inner = aways[k], inners[k]
        first = away * inner * (one < early_far).astype(jnp.int32)
        second = (1 - away) * inner * (two < early_near).astype(jnp.int32)
        slot = jnp.where(away == 1, jnp.where(first == 1, one, three), jnp.where(second == 1, early_far + two, four))
        one, two = one + first, two + second
        three, four = three + away - first, four + 1 - away - second
        slots[slot] = buffers[k]
        slots[total + slot] = k
    slots[2 * total] = early_far + early_near
    slots[2 * total + 1] = rest_far
    slots[2 * total + 2] = sends - early_far - early_near


def pick_tiles(snapshot, sizes, early, first, tile_pos, slots, numbers, main, strip, tables, xin, base):
    sends, per_row, half, blocks = sizes
    total = slot_count(sends, early)
    sub = lax.broadcasted_iota(jnp.int32, (8, 128), 0)
    channel = tables[8:16]
    def pick(slot):
        where = tile_pos[snapshot, slots[total + first + slot]]
        block = lax.div(where, per_row)
        lanes = pl.ds(pl.multiple_of(lax.rem(where, per_row) * TW, TW), TW)
        group = pl.ds(pl.multiple_of(lax.div(block, 2) * 8, 8), 8)
        edge = (block == 0) | (block == blocks - 1)
        beside = pl.ds(pl.multiple_of(jnp.where(block == 0, 16, 0), 8), 8)
        lower = lax.rem(block, 2) == 1

        def tile(x):
            return jnp.where(lower, pltpu.roll(x, TR, 0), x)

        def value(at):
            inside = main[at][group, lanes]
            if strip is None:
                return tile(inside)
            return tile(jnp.where(edge, strip[at][beside, lanes], inside))

        old = value(0)
        which = tile(numbers[group, lanes]).astype(jnp.int32)
        base[slot] = (old - value(1))[0:TR]
        for r in range(TR):
            found = jnp.take_along_axis(channel, jnp.broadcast_to(which[r : r + 1], (8, 128)), axis=1)
            xin[slot, r] = jnp.where(sub % 4 == 0, jnp.broadcast_to(old[r : r + 1], (8, 128)), found)

    last = xin.shape[0] - BATCH
    for slot in range(xin.shape[0]):
        if first == 0 or slot < last:
            pick(slot)
    if first:

        @pl.when(slots[2 * total + 2] > last)
        def _():
            for slot in range(last, xin.shape[0]):
                pick(slot)


def strip_coef(coef, outer, rows):
    return lambda k, cut: jnp.concatenate(
        [coef[k, rows - 8 : rows, cut], outer[k, :, cut], coef[k, 0:8, cut]], axis=0
    )


def first_strip_kernel(
    sizes, place, tile_pos, slots, both, ext, first, second, tables, coef, fields, xin, base, strip, outer, ids, work,
):
    rows, lanes = both.shape[1:]
    wide = lanes + EXT
    odd = lax.rem(place[0], 2) == 1
    above = jnp.where(odd, first[...], second[...])
    below = jnp.where(odd, second[...], first[...])
    none = jnp.zeros((2, wide), F32)
    ids[...] = jnp.concatenate([below[STEPS:], none, above[STEPS:]], axis=0).astype(jnp.int32)
    look_up(tables, ids, outer)
    work[0, 0:8, 0:lanes] = both[0, rows - 8 : rows]
    work[0, 0:8, lanes:wide] = ext[0, rows - 8 : rows]
    work[0, 8:16] = jnp.concatenate([below[:STEPS], above[:STEPS]], axis=0)
    work[0, 16:24, 0:lanes] = both[0, 0:8]
    work[0, 16:24, lanes:wide] = ext[0, 0:8]
    for step in range(2):
        source = work.at[step]
        target = work.at[1] if step == 0 else strip

        def write(cut, new):
            target[:, cut] = new

        advance(lambda cut: source[:, cut], strip_coef(coef, outer, rows), write, 24, wide // 128)
    main = (fields.at[0], fields.at[1])
    edge = (work.at[1], strip)
    pick_tiles(0, sizes, True, BATCH, tile_pos, slots, both.at[1], main, edge, tables, xin, base)


def second_strip_kernel(
    sizes, place, tile_pos, tile_dest, both, tables, coef, fields, strip, outer, final, xin, base, slots, work,
):
    rows, lanes = both.shape[1:]
    wide = lanes + EXT
    for step in range(2):
        source = strip if step == 0 else work.at[0]
        target = work.at[step]

        def write(cut, new):
            target[:, cut] = new

        advance(lambda cut: source[:, cut], strip_coef(coef, outer, rows), write, 24, wide // 128)
    sub = lax.broadcasted_iota(jnp.int32, (8, lanes), 0)
    final[0:8] = jnp.where(sub < STEPS, work[1, 16:24, 0:lanes], fields[3, 0:8, 0:lanes])
    final[8 : rows - 8] = fields[3, 8 : rows - 8, 0:lanes]
    final[rows - 8 : rows] = jnp.where(sub >= 8 - STEPS, work[1, 0:8, 0:lanes], fields[3, rows - 8 : rows, 0:lanes])
    order_tiles(1, sizes, False, place, tile_pos, tile_dest, slots)
    main = (fields.at[2], fields.at[3])
    edge = (work.at[0], work.at[1])
    pick_tiles(1, sizes, False, 0, tile_pos, slots, both.at[1], main, edge, tables, xin, base)


def split(x):
    high = x.astype(BF16)
    return high, (x - high.astype(F32)).astype(BF16)


def weights3(w):
    high = w.astype(BF16).astype(F32)
    return jnp.concatenate([high, high, w - high], axis=1).astype(BF16)


def values3(high, low):
    return jnp.concatenate([high, low, high], axis=0)


def times(a, b):
    return lax.dot_general(a, b, (((1,), (0,)), ((), ())), preferred_element_type=F32)


def over_cells(a, b):
    return lax.dot_general(a, b, (((1,), (1,)), ((), ())), preferred_element_type=F32)


def gelu_and_slope(z):
    square = z * z
    t = jnp.tanh(z * (GELU_A + (GELU_A * GELU_B) * square))
    gate = 0.5 + 0.5 * t
    value = z * gate
    return value, gate + (value - value * gate) * (2 * GELU_A + (6 * GELU_A * GELU_B) * square)


def lane_shift(x, by):
    lane = lax.broadcasted_iota(jnp.int32, x.shape, 1)
    return jnp.where(lane == (0 if by == 1 else TW - 1), 0.0, pltpu.roll(x, by % TW, 1))


def batch_gradients(cells, gaps, weights):
    w1, mix, w3, w3_t, mix_t = weights
    number = len(cells)
    zero8 = jnp.zeros((8, TW), F32)
    sub8 = lax.broadcasted_iota(jnp.int32, (8, TW), 0)
    columns = []
    for tile in cells:
        sides = [jnp.where(sub8 < 4, lane_shift(x, 1), lane_shift(x, -1)) for x in tile]
        sides = [zero8] + sides + [zero8]
        center = [zero8] + list(tile) + [zero8]
        for r in range(TR):
            stacked = []
            for dr in range(3):
                stacked += [sides[r + dr], center[r + dr]]
            columns.append(jnp.concatenate(stacked, axis=0))
    x_hi, x_lo = split(jnp.concatenate(columns, axis=1))
    h1, slope1 = gelu_and_slope(times(w1, values3(x_hi, x_lo)))
    h1_hi, h1_lo = split(h1)
    h2, slope2 = gelu_and_slope(times(mix, values3(h1_hi, h1_lo)))
    h2_hi, h2_lo = split(h2)
    taps = times(w3, values3(h2_hi, h2_lo))

    sub = lax.broadcasted_iota(jnp.int32, (16, TW), 0)
    tap_col, tap_row = lax.rem(sub, 3), lax.div(sub, 3)
    zero16 = jnp.zeros((16, TW), F32)

    def by_col(x, by):
        return jnp.where(
            tap_col == 0, lane_shift(x, by), jnp.where(tap_col == 2, lane_shift(x, -by), x)
        )

    def by_row(first, middle, last):
        return jnp.where(
            tap_row == 0, first, jnp.where(tap_row == 1, middle, jnp.where(tap_row == 2, last, 0.0))
        )

    spread = []
    for t in range(number):
        moved = [zero16]
        for r in range(TR):
            at = (t * TR + r) * TW
            moved.append(by_col(taps[:, at : at + TW], 1))
        moved.append(zero16)
        errors = [zero16]
        for r in range(TR):
            summed = jnp.sum(by_row(moved[r], moved[r + 1], moved[r + 2]), axis=0, keepdims=True)
            errors.append(by_col(jnp.broadcast_to(2.0 * (summed + gaps[t][r]), (16, TW)), -1))
        errors.append(zero16)
        spread += [by_row(errors[r + 2], errors[r + 1], errors[r]) for r in range(TR)]
    e_hi, e_lo = split(jnp.concatenate(spread, axis=1))
    d2_hi, d2_lo = split(times(w3_t, values3(e_hi, e_lo)) * slope2)
    d1_hi, d1_lo = split(times(mix_t, values3(d2_hi, d2_lo)) * slope1)

    result = []
    for t in range(number):
        own = slice(t * TR * TW, (t + 1) * TR * TW)
        both = lambda high, low: jnp.concatenate([high[:, own], low[:, own]], axis=0)
        result.append(
            jnp.concatenate(
                [
                    over_cells(both(d2_hi, d2_lo), both(h1_hi, h1_lo)),
                    over_cells(both(x_hi, x_lo), both(d1_hi, d1_lo)),
                    over_cells(both(e_hi, e_lo), both(h2_hi, h2_lo)),
                ],
                axis=0,
            )
        )
    return result


WEIGHTS = ((64, 144), (64, 192), (16, 192), (64, 48), (64, 192))


def prepare(params, weights):
    mix = jnp.concatenate([params[0:32, 0:64], params[0:32, 64:128]], axis=0)
    side, rest = params[32:56, 0:64], params[32:56, 64:128]
    none = jnp.zeros((8, 64), F32)
    taps = [[side[8 * r : 8 * r + 8], rest[4 * r : 4 * r + 4], none[0:4]] for r in range(3)]
    w1 = jnp.concatenate(sum(taps, []), axis=0)
    w3 = jnp.concatenate([rest[12:21], none[0:7]], axis=0)
    for ref, w in zip(weights, (w1.T, mix, w3, w3.T, mix.T)):
        ref[...] = weights3(w)


def add_batches(first, last, lead, number, masked, slots, xin, base, weights, total):
    weights = [ref[...] for ref in weights]

    def body(i, carry):
        at = [i * BATCH + k for k in range(BATCH)]
        cells = [[xin[j, r] for r in range(TR)] for j in at]
        gaps = [[base[j, r : r + 1, :] for r in range(TR)] for j in at]
        into = [slots[lead + j] for j in at]
        if masked:
            cells = [[jnp.where(j < number, x, 0.0) for x in tile] for j, tile in zip(at, cells)]
            gaps = [[jnp.where(j < number, x, 0.0) for x in tile] for j, tile in zip(at, gaps)]
        for buffer, grad in zip(into, batch_gradients(cells, gaps, weights)):
            total[buffer] += grad
        return carry

    lax.fori_loop(first, last, body, 0)


def fold(sums):
    def parts(first, height):
        x = sums[first : first + height, :] + sums[first + height : first + 2 * height, :]
        return x[:, 0:64] + x[:, 64:128]

    d_mix, d_w1, d_w3 = parts(0, 64), parts(128, 48), parts(224, 16)
    side = [d_w1[16 * r : 16 * r + 8] for r in range(3)]
    center = [d_w1[16 * r + 8 : 16 * r + 12] for r in range(3)]
    rest = jnp.concatenate(center + [d_w3[0:9], jnp.zeros((3, 64), F32)], axis=0)
    return jnp.concatenate(
        [
            jnp.concatenate([d_mix[0:32], d_mix[32:64]], axis=1),
            jnp.concatenate([jnp.concatenate(side, axis=0), rest], axis=1),
        ],
        axis=0,
    )


def batches(sends, early, slots):
    at = 2 * slot_count(sends, early)
    rest_far, rest = slots[at + 1], slots[at + 2]
    every = lax.div(rest + (BATCH - 1), BATCH)
    return jnp.maximum(lax.div(rest_far + (BATCH - 1), BATCH), every - 1), every, rest


def first_gradients(sends, early, slots, xin, base, weights, far, total):
    count, every, number = batches(sends, early, slots)
    masked = early or sends % BATCH != 0
    add_batches(0, count, lead_of(early), number, masked, slots, xin, base, weights, total)
    for b in range(far.shape[0]):
        far[b] = fold(total.at[b])


def first_gradient_kernel(sends, slots, xin, base, params, far, total, *weights):
    prepare(params, weights)
    total[...] = jnp.zeros_like(total)
    first_gradients(sends, False, slots, xin, base, weights, far, total)


def second_gradient_kernel(sends, early, slots, xin, base, begun, *rest):
    *weights, near, total = rest
    half = near.shape[0]
    total[half : 2 * half] = begun[half : 2 * half]
    count, every, number = batches(sends, early, slots)
    masked = early or sends % BATCH != 0
    add_batches(count, every, lead_of(early), number, masked, slots, xin, base, weights, total)
    for b in range(half):
        near[b] = fold(total.at[half + b])


def opening_kernel(sizes, place, tile_pos, tile_dest, both, ext, tables, params, fields, coef, slots, begun, *rest):
    *weights, xin, base, ids, start = rest
    prepare(params, weights)
    inner_kernel(sizes, place, tile_pos, tile_dest, both, ext, tables, fields, coef, xin, base, slots, ids, start)
    begun[...] = jnp.zeros_like(begun)
    number = slots[2 * slot_count(sizes[0], True)]
    add_batches(0, jnp.minimum(number, 1), 0, number, True, slots, xin, base, weights, begun)


def edge_kernel(sizes, place, tile_pos, slots, both, ext, first, second, tables, coef, fields, begun, *rest):
    *weights, xin, base, strip, outer, far, total, ids, work = rest
    first_strip_kernel(
        sizes, place, tile_pos, slots, both, ext, first, second, tables, coef, fields, xin, base, strip, outer, ids, work
    )
    total[...] = begun[...]
    first_gradients(sizes[0], True, slots, xin, base, weights, far, total)


def combine_kernel(entries, own, other, out):
    result = jnp.zeros(out.shape, F32)
    for b in range(own.shape[0]):
        full = own[b] + other[b]
        square = jnp.sum(full * full, keepdims=True)
        result = result + full * lax.rsqrt(square / entries + NORM_EPS)
    out[...] = result


def pack_weights(conv_in, mix_weight, conv_out):
    taps = jnp.transpose(conv_in, (0, 2, 1)).reshape(3, 3, 4, conv_in.shape[1])
    side = jnp.concatenate([taps[:, 0], taps[:, 2]], axis=1).reshape(24, conv_in.shape[1])
    rest = jnp.concatenate(
        [taps[:, 1].reshape(12, conv_in.shape[1]), jnp.pad(conv_out[:, 0, :], ((0, 3), (0, 0)))], axis=0
    )
    mix = jnp.concatenate([mix_weight[0:32], mix_weight[32:64]], axis=1)
    return jnp.concatenate([mix, jnp.concatenate([side, rest], axis=1)], axis=0)


def unpack_kernel(one, other, conv_in, mix, conv_out):
    mix_rows = mix.shape[0] // 2
    for k in range(2):
        at = slice(64 * k, 64 * k + 64)
        mix[mix_rows * k : mix_rows * (k + 1)] = one[0:mix_rows, at] + other[0:mix_rows, at]
    side = one[32:56, 0:64] + other[32:56, 0:64]
    rest = one[32:56, 64:128] + other[32:56, 64:128]
    for r in range(3):
        conv_in[3 * r] = side[8 * r : 8 * r + 4]
        conv_in[3 * r + 1] = rest[4 * r : 4 * r + 4]
        conv_in[3 * r + 2] = side[8 * r + 4 : 8 * r + 8]
    for k in range(9):
        conv_out[k] = rest[12 + k : 13 + k]


def local(
    initial_field,
    coef_index,
    kappa_table,
    drift_table,
    tile_pos,
    tile_dest,
    conv_in,
    mix_weight,
    conv_out,
):
    rows, lanes = initial_field.shape
    solvers = lax.axis_size("solver")
    trainers = lax.axis_size("trainer")
    half = solvers // 2
    j = lax.axis_index("solver")
    t = lax.axis_index("trainer")
    sends = tile_pos.shape[-1]
    entries = conv_in.size + mix_weight.size + conv_out.size

    def swap(x, axis, bit):
        count = lax.axis_size(axis)
        return lax.ppermute(x, axis, [(i, i ^ bit) for i in range(count)])

    place = j.reshape(1)
    tile_pos = tile_pos.reshape(SNAPS, sends)
    tile_dest = tile_dest.reshape(SNAPS, sends)
    both = lax.optimization_barrier(jnp.stack([initial_field, (coef_index + 1).astype(F32)]))
    ext = swap(jnp.where(t == 0, both[:, :, lanes - EXT :], both[:, :, :EXT]), "trainer", 1)
    lane = lax.broadcasted_iota(jnp.int32, ext.shape, 2)
    ext = jnp.where((lane < LIVE) == (t == 0), ext, 0.0)

    def edge_rows(bottom):
        def part(k, height):
            start = jnp.where(bottom, rows - height, 0)
            own = lax.dynamic_slice_in_dim(both[k], start, height, 0)
            return jnp.concatenate([own, lax.dynamic_slice_in_dim(ext[k], start, height, 0)], axis=1)

        return jnp.concatenate([part(0, STEPS), part(1, STEPS - 1)], axis=0)

    odd = j % 2 == 1
    inner = [(i, i ^ 1) for i in range(solvers)]
    outer_pairs = []
    for i in range(solvers):
        beside = i + 1 if i % 2 else i - 1
        for k in range(trainers):
            there = beside * trainers + k if 0 <= beside < solvers else i * trainers + (k ^ 1)
            outer_pairs.append((i * trainers + k, there))
    first = lax.ppermute(edge_rows(~odd), "solver", inner)
    second = lax.ppermute(edge_rows(odd), ("solver", "trainer"), outer_pairs)
    second = jnp.where((j == 0) | (j == solvers - 1), 0.0, second)

    vr, vc = drift_table[0], drift_table[1]
    tables = jnp.stack(
        [
            kappa_table + jnp.maximum(vr, 0.0),
            kappa_table - jnp.minimum(vr, 0.0),
            kappa_table + jnp.maximum(vc, 0.0),
            kappa_table - jnp.minimum(vc, 0.0),
        ]
    )
    none = jnp.zeros_like(kappa_table)
    channel = jnp.stack([none, kappa_table, vr, vc, none, kappa_table, vr, vc])
    fill = 127 - kappa_table.shape[0]
    tables = jnp.pad(jnp.concatenate([tables, jnp.zeros_like(tables), channel]), ((0, 0), (1, fill)))

    sizes = (sends, lanes // TW, half, rows // TR)
    wide = lanes + EXT
    def tile_shapes(number):
        return (
            jax.ShapeDtypeStruct((number, TR, 8, TW), F32),
            jax.ShapeDtypeStruct((number, TR, TW), F32),
        )

    def slots_shape(early):
        return jax.ShapeDtypeStruct((2 * slot_count(sends, early) + 3,), jnp.int32)

    held = slot_count(sends, False)
    params = pack_weights(conv_in, mix_weight, conv_out)
    changes = []
    work = 3 * 2 * 20000 * TR * TW * sends // 2
    folded = jax.ShapeDtypeStruct((half,) + params.shape, F32)
    totals = jax.ShapeDtypeStruct((2 * half, 256, 128), F32)

    prepared = tuple(jax.ShapeDtypeStruct(shape, BF16) for shape in WEIGHTS)

    def room(shape):
        return pltpu.VMEM(shape.shape, shape.dtype)

    fields, coef, slots, begun, *weights = pl.pallas_call(
        functools.partial(opening_kernel, sizes),
        out_shape=(
            jax.ShapeDtypeStruct((STEPS, rows, wide), F32),
            jax.ShapeDtypeStruct((4, rows, wide), F32),
            slots_shape(True),
            totals,
        )
        + prepared,
        in_specs=[SMEM] * 3 + [VMEM] * 4,
        out_specs=(VMEM, VMEM, SMEM, VMEM) + (VMEM,) * len(prepared),
        scratch_shapes=[room(x) for x in tile_shapes(BATCH)]
        + [pltpu.VMEM((rows, wide), jnp.int32), pltpu.VMEM((rows, wide), F32)],
        compiler_params=PARAMS,
        cost_estimate=pl.CostEstimate(flops=1 << 31, bytes_accessed=1 << 23, transcendentals=0),
    )(place, tile_pos, tile_dest, both, ext, tables, params)

    def gradients(kernel, tiles, others, out_shape, scratch):
        xin, base, slots = tiles
        return pl.pallas_call(
            kernel,
            out_shape=out_shape,
            in_specs=[SMEM] + [VMEM] * (2 + len(others)),
            out_specs=jax.tree.map(lambda _: VMEM, out_shape),
            scratch_shapes=scratch,
            compiler_params=PARAMS,
            cost_estimate=pl.CostEstimate(flops=work * 16, bytes_accessed=1 << 21, transcendentals=1 << 20),
        )(slots, xin, base, *others)

    xin, base, strip, outer, far, begun = pl.pallas_call(
        functools.partial(edge_kernel, sizes),
        out_shape=tile_shapes(held)
        + (jax.ShapeDtypeStruct((24, wide), F32), jax.ShapeDtypeStruct((4, 8, wide), F32), folded, totals),
        in_specs=[SMEM] * 3 + [VMEM] * (8 + len(weights)),
        out_specs=(VMEM,) * 6,
        scratch_shapes=[pltpu.VMEM((8, wide), jnp.int32), pltpu.VMEM((2, 24, wide), F32)],
        compiler_params=PARAMS,
    )(place, tile_pos, slots, both, ext, first, second, tables, coef, fields, begun, *weights)

    def second_part(fields, strip):
        return pl.pallas_call(
            functools.partial(second_strip_kernel, sizes),
            out_shape=(jax.ShapeDtypeStruct((rows, lanes), F32),) + tile_shapes(held) + (slots_shape(False),),
            in_specs=[SMEM] * 3 + [VMEM] * 6,
            out_specs=(VMEM,) * 3 + (SMEM,),
            scratch_shapes=[pltpu.VMEM((2, 24, wide), F32)],
            compiler_params=PARAMS,
            cost_estimate=pl.CostEstimate(flops=1 << 31, bytes_accessed=1 << 23, transcendentals=0),
        )(place, tile_pos, tile_dest, both, tables, coef, fields, strip, outer)

    tiles = (xin, base, slots)
    for snapshot in range(SNAPS):
        early = snapshot == 0
        if not early:
            far, begun, *weights = gradients(
                functools.partial(first_gradient_kernel, sends), tiles, [params], (folded, totals) + prepared, []
            )
        arrived = swap(far, "solver", half)
        near = gradients(
            functools.partial(second_gradient_kernel, sends, early), tiles, [begun, *weights], folded, [room(totals)]
        )
        near = near + arrived
        bit = 1
        while 2 * bit < half:
            near = near + swap(near, "solver", bit)
            bit = 2 * bit
        if snapshot == 0:
            near, fields, strip = lax.optimization_barrier((near, fields, strip))
            final, *tiles = second_part(fields, strip)
        direction = pl.pallas_call(
            functools.partial(combine_kernel, entries),
            out_shape=jax.ShapeDtypeStruct(params.shape, F32),
            in_specs=[VMEM] * 2,
            out_specs=VMEM,
            compiler_params=PARAMS,
        )(near, swap(near, "solver", bit))
        if snapshot == 0:
            direction, *tiles = lax.optimization_barrier((direction, *tiles))
        across = [(i, i ^ (half * trainers + 1)) for i in range(solvers * trainers)]
        direction = direction + lax.ppermute(direction, ("solver", "trainer"), across)
        direction = direction + swap(direction, "trainer", 1)
        direction = direction / (solvers * trainers)
        changes.append(direction)
        params = params - STEP_RATE * direction
    first, mix, last = pl.pallas_call(
        unpack_kernel,
        out_shape=tuple(jax.ShapeDtypeStruct(w.shape, F32) for w in (jnp.transpose(conv_in, (0, 2, 1)), mix_weight, conv_out)),
        in_specs=[VMEM] * 2,
        out_specs=(VMEM,) * 3,
        compiler_params=PARAMS,
    )(*changes)
    return (final, jnp.transpose(first, (0, 2, 1)), mix, last)


def solution(mesh):
    return jax.shard_map(
        local,
        mesh=mesh,
        in_specs=(
            P(("groups", "solver"), "trainer"),
            P(("groups", "solver"), "trainer"),
            P("groups"),
            P("groups", None),
            P("groups", "solver", "trainer", None),
            P("groups", "solver", "trainer", None, None),
            P("groups", None, None),
            P("groups", None),
            P("groups", None, None),
        ),
        out_specs=(
            P(("groups", "solver"), "trainer"),
            P("groups", None, None),
            P("groups", None),
            P("groups", None, None),
        ),
        check_vma=False,
    )
```
